256 devices in a mesh: dp: 8 (over y, core), row: 4 (over x), col: 8 (over z).
Axes of the slice: x: 4, y: 4, z: 8, core: 2. Of those that a mesh axis runs over, the one named last changes fastest.
Arguments:
- activations: bfloat16 [12288, 4096], P('dp', 'row'), may hold values from -12.7 to 12.7
- cotangent: bfloat16 [12288, 16384], P('dp', 'col'), may hold values from -0.11456794 to 0.11456794
- param: float32 [4096, 16384], P('row', ('col', 'dp')), may hold values from -6 to 6
- row_state: float32 [4096], P('row'), may hold values from 0.02 to 0.3
- col_state: float32 [16384], P(('col', 'dp')), may hold values from 0.02 to 0.3
Outputs:
- new_param: float32 [4096, 16384], P('row', ('col', 'dp'))
- new_row: float32 [4096], P('row')
- new_col: float32 [16384], P(('col', 'dp'))
The draws below stay inside these ranges and needn't reach their ends.
All inputs are finite; a program needn't handle non-finite values.
Results may differ from the reference program's by a relative error of at most 0.0003.
Values may be sent and summed in bfloat16 or wider, within the bound.
No kernel may reach another device: no remote copies, remote signals or barrier semaphores. Data moves between devices by JAX's collectives and lax.ppermute only.
A program may use at most 128 MiB of HBM per device.

```python
import math
import jax
import jax.numpy as jnp
from jax import lax

D = 4096
FF = 16384
TOKENS = 12288


def draw_activations(key, part):
    key = jax.random.fold_in(key, 11)
    base = jnp.clip(jax.random.normal(key, (TOKENS, D), jnp.float32), -4.0, 4.0)
    spread = 0.5
    level = jnp.power(10.0, spread * jnp.arange(D, dtype=jnp.float32) / D)
    return (base * level[None, :]).astype(jnp.bfloat16)


def draw_cotangent(key, part):
    key = jax.random.fold_in(key, 23)
    base = jnp.clip(jax.random.normal(key, (TOKENS, FF), jnp.float32), -4.0, 4.0)
    spread = 0.5
    level = jnp.power(10.0, spread * jnp.arange(FF, dtype=jnp.float32) / FF)
    return (base * level[None, :] / jnp.sqrt(jnp.float32(TOKENS))).astype(jnp.bfloat16)


def shard_levels(key, extent, shards, smallest, high):
    level, own = 1.0, jax.random.fold_in(key, 6)
    for position, shards_of in shards:
        draws = jnp.exp(jax.random.uniform(jax.random.fold_in(own, position), (shards_of,), jnp.float32, smallest / len(shards), high / len(shards)))
        level = level * jnp.repeat(draws, extent[position] // shards_of).reshape([-1 if axis == position else 1 for axis in range(len(extent))])
    return level


def bell_draw(own_key, extent, scale, most, cuts=(), kind=jnp.bfloat16):
    drawn = jax.random.normal(own_key, extent, jnp.float32) * scale
    if len(cuts) > 0:
        drawn = shard_levels(own_key, extent, cuts, -0.22, 0.18) * drawn
    return jnp.clip(drawn, min=-most, max=most).astype(kind)


def setup_inputs(seed: int = 0) -> dict:
    splits = jax.random.split(jax.random.key(seed), 6)
    activations = draw_activations(jax.random.fold_in(splits[5], 71), 0)
    cotangent = draw_cotangent(jax.random.fold_in(splits[5], 71), 0)
    param = bell_draw(splits[2], (D, FF), 1.0, 6.0, ((0, 4), (1, 64)), jnp.float32)
    row_state = jnp.clip(jnp.exp(math.log(0.3) - 2.7080503 * jax.random.uniform(splits[3], (D,), jnp.float32) ** shard_levels(splits[3], (D,), ((0, 4),), -0.2, 0.2)), 0.02, 0.3)
    col_state = jnp.clip(jnp.exp(math.log(0.3) - 2.7080503 * jax.random.uniform(splits[4], (FF,), jnp.float32) ** shard_levels(splits[4], (FF,), ((0, 64),), -0.2, 0.2)), 0.02, 0.3)
    return {"activations": activations, "cotangent": cotangent, "param": param, "row_state": row_state, "col_state": col_state}


decay_rate = 0.9
step_size = 0.3

def reference(activations, cotangent, param, row_state, col_state):
    gradient = lax.dot_general(activations, cotangent, (((0,), (0,)), ((), ())), preferred_element_type=jnp.float32)
    squares = gradient * gradient
    new_row = decay_rate * row_state + (1.0 - decay_rate) * lax.optimization_barrier(jnp.mean(squares, axis=1))
    new_col = decay_rate * col_state + (1.0 - decay_rate) * lax.optimization_barrier(jnp.mean(squares, axis=0))
    row_level = jnp.mean(new_row)
    update = gradient * lax.rsqrt(new_row[:, None] * new_col[None, :] / row_level)
    clip = jnp.maximum(1.0, jnp.sqrt(jnp.mean(update * update)))
    scale = jnp.sqrt(jnp.mean(param * param))
    new_param = param - step_size * scale * update / clip
    return (new_param, new_row, new_col)
```

```python
import jax
import jax.numpy as jnp
from jax import lax
from jax.sharding import Mesh, PartitionSpec as P

D = 4096
FF = 16384

decay_rate = 0.9
step_size = 0.3

Y, C, X, Z = 4, 2, 4, 8
OWN = 256
HALF = 512
WIRE = jnp.float16

swap_core = [(0, 1), (1, 0)]
to_left = [(i, (i - 1) % Y) for i in range(Y)]
to_right = [(i, (i + 1) % Y) for i in range(Y)]
pair_near = [(i, i ^ 1) for i in range(X)]
pair_wrap = [(i, X - 1 - i) for i in range(X)]


def sum_over_x(value):
    value = value + lax.ppermute(value, "x", pair_near)
    return value + lax.ppermute(value, "x", pair_wrap)


def per_device(activations, cotangent, param, row_state, col_state):
    y = lax.axis_index("y")
    c = lax.axis_index("c")

    def partial(owner_y, owner_c):
        start = (lax.rem(owner_y + Y, Y) * C + owner_c) * OWN
        block = lax.dynamic_slice_in_dim(cotangent, start, OWN, axis=1)
        return lax.dot_general(
            activations, block, (((0,), (0,)), ((), ())), preferred_element_type=jnp.float32
        )

    def chip_sum(owner_y):
        away = partial(owner_y, 1 - c).astype(WIRE)
        came = lax.ppermute(away, "c", swap_core)
        return partial(owner_y, c) + came.astype(jnp.float32)

    far = chip_sum(y + 2).astype(WIRE)
    far_left = lax.ppermute(far[:HALF], "y", to_left)
    far_right = lax.ppermute(far[HALF:], "y", to_right)
    left = chip_sum(y - 1)
    right = chip_sum(y + 1)
    near_left = lax.ppermute(left[HALF:].astype(WIRE), "y", to_left)
    near_right = lax.ppermute(right[:HALF].astype(WIRE), "y", to_right)
    own = chip_sum(y)
    last_left = lax.ppermute((left[:HALF] + far_left).astype(WIRE), "y", to_left)
    last_right = lax.ppermute((right[HALF:] + far_right).astype(WIRE), "y", to_right)
    top = own[:HALF] + near_right.astype(jnp.float32) + last_left.astype(jnp.float32)
    low = own[HALF:] + near_left.astype(jnp.float32) + last_right.astype(jnp.float32)
    gradient = jnp.concatenate([top, low], axis=0)

    squares = gradient * gradient
    row_part = jnp.sum(squares, axis=1)
    col_part = jnp.sum(squares, axis=0)
    new_col = decay_rate * col_state + (1.0 - decay_rate) * sum_over_x(col_part) / D
    weighted = jnp.sum(squares * (1.0 / new_col)[None, :], axis=1)
    param_part = jnp.sum(param * param)
    packed = jnp.concatenate(
        [row_part.reshape(8, 128), weighted.reshape(8, 128), jnp.full((8, 128), param_part)]
    )
    packed = packed + lax.ppermute(packed, "c", swap_core)
    spread = jnp.broadcast_to(packed[None], (Y * Z,) + packed.shape)
    packed = jnp.sum(lax.all_to_all(spread, ("y", "z"), 0, 0, tiled=True), axis=0)
    row_total = packed[:8].reshape(1024)
    weighted_total = packed[8:16].reshape(1024)
    new_row = decay_rate * row_state + (1.0 - decay_rate) * row_total / FF
    sums = jnp.stack([jnp.sum(weighted_total / new_row), jnp.sum(new_row), packed[16, 0]])
    sums = sum_over_x(jnp.broadcast_to(sums[:, None], (3, 128)))
    row_level = sums[1, 0] / D
    entries = D * FF
    clip = jnp.maximum(1.0, jnp.sqrt(row_level * sums[0, 0] / entries))
    scale = jnp.sqrt(sums[2, 0] / entries)
    factor = step_size * scale * jnp.sqrt(row_level) / clip
    update = gradient * (factor * lax.rsqrt(new_row))[:, None] * lax.rsqrt(new_col)[None, :]
    return (param - update, new_row, new_col)


def solution(mesh):
    split = Mesh(mesh.devices.reshape(Y, C, X, Z), ("y", "c", "x", "z"))
    tokens = ("y", "c")
    columns = ("z", "y", "c")
    in_specs = (P(tokens, "x"), P(tokens, "z"), P("x", columns), P("x"), P(columns))
    out_specs = (P("x", columns), P("x"), P(columns))
    return jax.shard_map(
        per_device, mesh=split, in_specs=in_specs, out_specs=out_specs, check_vma=False
    )
```

```python
import jax
import jax.numpy as jnp
from jax import lax
from jax.experimental import pallas as pl
from jax.experimental.pallas import tpu as pltpu
from jax.sharding import Mesh, PartitionSpec as P

D = 4096
FF = 16384
TOKENS = 12288

decay_rate = 0.9
step_size = 0.3

Y, C, X, Z = 4, 2, 4, 8
ROWS = D // X
OWN = FF // (Z * Y * C)
DEPTH = TOKENS // (Y * C)
HALF = ROWS // 2
LANES = 128
GROUPS = ROWS // LANES
SHARE = GROUPS // C
STEPS = 3
WIRE = jnp.float16
F32 = jnp.float32
BF16 = jnp.bfloat16
TILE = (8, LANES)

swap_core = [(0, 1), (1, 0)]
to_left = [(i, (i - 1) % Y) for i in range(Y)]
to_right = [(i, (i + 1) % Y) for i in range(Y)]
pair_near = [(i, i ^ 1) for i in range(X)]
pair_wrap = [(i, X - 1 - i) for i in range(X)]

VMEM = pl.BlockSpec(memory_space=pltpu.VMEM)
SMEM = pl.BlockSpec(memory_space=pltpu.SMEM)
LIMIT = 14 * 2**20


def call(kernel, name, outs, *operands, scalars=0, micros=1):
    return pl.pallas_call(
        kernel,
        name=name,
        in_specs=[SMEM] * scalars + [VMEM] * (len(operands) - scalars),
        out_specs=[VMEM] * len(outs),
        out_shape=[jax.ShapeDtypeStruct(shape, kind) for shape, kind in outs],
        compiler_params=pltpu.CompilerParams(vmem_limit_bytes=LIMIT),
        cost_estimate=pl.CostEstimate(
            flops=0, bytes_accessed=micros * 2 * 2**20, transcendentals=0
        ),
    )(*operands)


def matmul_kernel(place, activations, block, out):
    del place
    step = pl.program_id(0)
    depth = block.shape[0]
    rows = activations[pl.ds(pl.multiple_of(step * depth, depth), depth), :]
    product = lax.dot_general(
        rows, block[...], (((0,), (0,)), ((), ())), preferred_element_type=F32
    )

    @pl.when(step == 0)
    def first():
        out[...] = product

    @pl.when(step > 0)
    def later():
        out[...] += product


def block_matmul(place, activations, cotangent):
    return pl.pallas_call(
        matmul_kernel,
        name="block_matmul",
        grid_spec=pltpu.PrefetchScalarGridSpec(
            num_scalar_prefetch=1,
            grid=(STEPS,),
            in_specs=[VMEM, pl.BlockSpec((DEPTH // STEPS, OWN), lambda k, place: (k, place[0]))],
            out_specs=pl.BlockSpec((ROWS, OWN), lambda k, place: (0, 0)),
        ),
        out_shape=jax.ShapeDtypeStruct((ROWS, OWN), F32),
        compiler_params=pltpu.CompilerParams(vmem_limit_bytes=LIMIT),
        cost_estimate=pl.CostEstimate(
            flops=2 * DEPTH * ROWS * OWN, bytes_accessed=2 * DEPTH * OWN, transcendentals=0
        ),
    )(place, activations, cotangent)


def lane_sums(block):
    folded = block[:, :LANES] + block[:, LANES:]
    return jnp.sum(folded.T, axis=0, keepdims=True)


def square_sum_kernel(param, out):
    value = param[...]
    out[...] = jnp.full(TILE, jnp.sum(value * value))


def row_sums_kernel(core, top, low, col_a, col_b, col_state, param_sum, new_col, mine, away):
    col = decay_rate * col_state[...] + (1.0 - decay_rate) * (col_a[...] + col_b[...]) / D
    new_col[...] = col
    inverse = 1.0 / col
    first = core[0] == 0
    for group in range(SHARE):
        sums = []
        for part in (top, low):
            block = part[group * LANES : (group + 1) * LANES, :]
            squares = block * block
            sums.append((lane_sums(squares), lane_sums(squares * inverse)))
        for k in range(2):
            at = k * SHARE + group
            mine[at : at + 1, :] = jnp.where(first, sums[0][k], sums[1][k])
            away[at : at + 1, :] = jnp.where(first, sums[1][k], sums[0][k])
    mine[2 * SHARE :, :] = param_sum[...]
    away[2 * SHARE :, :] = param_sum[...]


def message_kernel(mine, came, out):
    packed = mine[...] + came[...]
    high = packed.astype(BF16)
    rest = (packed - high.astype(F32)).astype(BF16)
    pieces = [
        high[:SHARE],
        rest[:SHARE],
        high[SHARE : 2 * SHARE],
        high[2 * SHARE : 2 * SHARE + 2],
        rest[2 * SHARE : 2 * SHARE + 2],
    ]
    message = jnp.concatenate([piece.astype(F32) for piece in pieces], axis=0).astype(BF16)
    for k in range(Y * Z):
        out[k] = message


def reduce_kernel(core, came, row_state, out):
    total = jnp.sum(came[...].astype(F32), axis=0)
    squares = total[:SHARE] + total[SHARE : 2 * SHARE]
    weighted = total[2 * SHARE : 3 * SHARE]
    state = jnp.where(core[0] == 0, row_state[:SHARE, :], row_state[SHARE:, :])
    row = decay_rate * state + (1.0 - decay_rate) * squares / FF
    param_total = total[3 * SHARE : 3 * SHARE + 1] + total[3 * SHARE + 2 : 3 * SHARE + 3]
    out[:SHARE, :] = row
    out[SHARE : SHARE + 1, :] = jnp.full((1, LANES), jnp.sum(weighted / row))
    out[SHARE + 1 : SHARE + 2, :] = jnp.full((1, LANES), jnp.sum(row))
    out[SHARE + 2 :, :] = jnp.broadcast_to(0.5 * param_total, (2, LANES))


def merge_kernel(core, mine, twin, new_row, scalars):
    first = core[0] == 0
    a, b = mine[:SHARE, :], twin[:SHARE, :]
    new_row[:SHARE, :] = jnp.where(first, a, b)
    new_row[SHARE:, :] = jnp.where(first, b, a)
    scalars[...] = mine[...] + twin[...]


def normalise_kernel(top, low, new_row, new_col, update):
    col_factor = lax.rsqrt(new_col[...])
    row_factor = lax.rsqrt(new_row[...])
    for group in range(GROUPS):
        part = top if group < SHARE else low
        at = group % SHARE
        block = part[at * LANES : (at + 1) * LANES, :]
        along = jnp.broadcast_to(row_factor[group : group + 1, :], (LANES, LANES)).T
        factor = jnp.concatenate([along, along], axis=1) * col_factor
        update[group * LANES : (group + 1) * LANES, :] = block * factor


def step_kernel(scalars_a, scalars_b, param, update, new_param):
    sums = scalars_a[...] + scalars_b[...]
    entries = D * FF
    row_level = sums[SHARE + 1 : SHARE + 2] / D
    clip = jnp.maximum(1.0, jnp.sqrt(row_level * sums[SHARE : SHARE + 1] / entries))
    scale = jnp.sqrt(sums[SHARE + 2 : SHARE + 3] / entries)
    factor = step_size * scale * jnp.sqrt(row_level) / clip
    factor = jnp.concatenate([factor, factor], axis=1)
    new_param[...] = param[...] - factor * update[...]


def per_device(activations, cotangent, param, row_state, col_state):
    y = lax.axis_index("y")
    c = lax.axis_index("c")
    barrier = lax.optimization_barrier
    places = [
        ((lax.rem(y + hop, Y) * C) + core)[None] for hop in (2, 3, 1, 0) for core in (1 - c, c)
    ]
    *places, core = barrier((*places, c[None]))

    def partial(place):
        return block_matmul(place, activations, cotangent)

    def swapped(place):
        return lax.ppermute(partial(place), "c", swap_core)

    def wide(value):
        return value.astype(F32)

    far_came = swapped(places[0])
    far_own = partial(places[1])
    far_top = barrier((far_own[:HALF] + far_came[:HALF]).astype(WIRE))
    far_low = barrier((far_own[HALF:] + far_came[HALF:]).astype(WIRE))
    far_left = lax.ppermute(far_top, "y", to_left)
    far_right = lax.ppermute(far_low, "y", to_right)
    *places, _, _ = barrier((*places, far_top, far_low))
    left_came = swapped(places[2])
    right_came = swapped(places[4])
    left = partial(places[3])
    right = partial(places[5])
    near_low = barrier((left[HALF:] + left_came[HALF:]).astype(WIRE))
    near_top = barrier((right[:HALF] + right_came[:HALF]).astype(WIRE))
    near_left = lax.ppermute(near_low, "y", to_left)
    near_right = lax.ppermute(near_top, "y", to_right)
    *places, _, _ = barrier((*places, near_low, near_top))
    own_came = swapped(places[6])
    own = partial(places[7])
    last_top = (left[:HALF] + left_came[:HALF] + wide(far_left)).astype(WIRE)
    last_low = (right[HALF:] + right_came[HALF:] + wide(far_right)).astype(WIRE)
    last_left = lax.ppermute(barrier(last_top), "y", to_left)
    last_right = lax.ppermute(barrier(last_low), "y", to_right)
    top = own[:HALF] + own_came[:HALF] + wide(near_right) + wide(last_left)
    low = own[HALF:] + own_came[HALF:] + wide(near_left) + wide(last_right)

    (param_sum,) = call(square_sum_kernel, "square_sum", [(TILE, F32)], param)
    col_part = jnp.sum(top * top, axis=0) + jnp.sum(low * low, axis=0)
    col_part = col_part.reshape(1, OWN)
    col_part = col_part + lax.ppermute(col_part, "x", pair_near)
    col_came = lax.ppermute(col_part, "x", pair_wrap)
    new_col, mine, away = call(
        row_sums_kernel,
        "row_sums",
        [((1, OWN), F32), ((2 * 8, LANES), F32), ((2 * 8, LANES), F32)],
        core,
        top,
        low,
        col_part,
        col_came,
        col_state.reshape(1, OWN),
        param_sum,
        scalars=1,
    )
    came = lax.ppermute(away, "c", swap_core)
    (message,) = call(message_kernel, "message", [((Y * Z, 16, LANES), BF16)], mine, came)
    came = lax.all_to_all(message, ("y", "z"), 0, 0, tiled=True)
    (reduced,) = call(
        reduce_kernel,
        "row_reduce",
        [(TILE, F32)],
        core,
        came,
        row_state.reshape(TILE),
        scalars=1,
    )
    twin = lax.ppermute(reduced, "c", swap_core)
    new_row, scalars = call(
        merge_kernel, "merge", [(TILE, F32), (TILE, F32)], core, reduced, twin, scalars=1
    )
    scalars = scalars + lax.ppermute(scalars, "x", pair_near)
    scalars_came = lax.ppermute(scalars, "x", pair_wrap)
    (update,) = call(
        normalise_kernel, "normalise", [((ROWS, OWN), F32)], top, low, new_row, new_col
    )
    (new_param,) = call(
        step_kernel, "step", [((ROWS, OWN), F32)], scalars, scalars_came, param, update
    )
    return (new_param, new_row.reshape(ROWS), new_col.reshape(OWN))


def solution(mesh):
    split = Mesh(mesh.devices.reshape(Y, C, X, Z), ("y", "c", "x", "z"))
    tokens = ("y", "c")
    columns = ("z", "y", "c")
    in_specs = (P(tokens, "x"), P(tokens, "z"), P("x", columns), P("x"), P(columns))
    out_specs = (P("x", columns), P("x"), P(columns))
    return jax.shard_map(
        per_device, mesh=split, in_specs=in_specs, out_specs=out_specs, check_vma=False
    )
```

```python
import jax
import jax.numpy as jnp
from jax import lax
from jax.experimental import pallas as pl
from jax.experimental.pallas import tpu as pltpu
from jax.sharding import Mesh, PartitionSpec as P

D = 4096
FF = 16384
TOKENS = 12288

decay_rate = 0.9
step_size = 0.3

Y, C, X, Z = 4, 2, 4, 8
ROWS = D // X
OWN = FF // (Z * Y * C)
DEPTH = TOKENS // (Y * C)
LANES = 128
GROUPS = ROWS // LANES
SHARE = GROUPS // C
STEPS = 6
WIRE = jnp.float16
F32 = jnp.float32
BF16 = jnp.bfloat16
TILE = (8, LANES)
TILE32 = (TILE, F32)

swap_core = [(0, 1), (1, 0)]
turn = (-1, 1)
to_ahead = [(i * C + k, (i + turn[k]) % Y * C + k) for i in range(Y) for k in range(C)]
to_behind = [(i * C + k, (i - turn[k]) % Y * C + k) for i in range(Y) for k in range(C)]
pair_near = [(i, i ^ 1) for i in range(X)]
pair_wrap = [(i, X - 1 - i) for i in range(X)]

VMEM = pl.BlockSpec(memory_space=pltpu.VMEM)
SMEM = pl.BlockSpec(memory_space=pltpu.SMEM)
HBM = pl.BlockSpec(memory_space=pltpu.HBM)
LIMIT = 14 * 2**20
FIRST_LIMIT = 48 * 2**20
SECOND_LIMIT = 43 * 2**20
THIRD_LIMIT = 39 * 2**20
NO_COST = pl.CostEstimate(flops=1, bytes_accessed=1, transcendentals=0)


def call(kernel, name, outs, *operands, scalars=0):
    return pl.pallas_call(
        kernel,
        name=name,
        in_specs=[SMEM] * scalars + [VMEM] * (len(operands) - scalars),
        out_specs=[VMEM] * len(outs),
        out_shape=[jax.ShapeDtypeStruct(shape, kind) for shape, kind in outs],
        compiler_params=pltpu.CompilerParams(vmem_limit_bytes=LIMIT),
        cost_estimate=NO_COST,
    )(*operands)


def load_rows(k):
    return pl.ds(k * DEPTH // STEPS, DEPTH // STEPS)


def pair_copies(owner, cotangent, pair, landed):
    width = C * OWN
    columns = pl.ds(pl.multiple_of(owner * width, width), width)
    return [
        pltpu.make_async_copy(
            cotangent.at[load_rows(k), columns], pair.at[load_rows(k), :], landed.at[k]
        )
        for k in range(STEPS)
    ]


def start_all(copies):
    for copy in copies:
        copy.start()


def wait_all(copies):
    for copy in copies:
        copy.wait()


def product(left, right):
    return lax.dot_general(left, right, (((0,), (0,)), ((), ())), preferred_element_type=F32)


def core_columns(core):
    return pl.ds(pl.multiple_of(core * OWN, OWN), OWN)


def first_kernel(owner, core, activations, cotangent, out, kept, pair, arrived, landed):
    blocks = pair_copies(owner[0], cotangent, pair, landed)
    wholes = [
        pltpu.make_async_copy(
            activations.at[load_rows(k), :], kept.at[load_rows(k), :], arrived.at[k]
        )
        for k in range(STEPS)
    ]
    for block, whole in zip(blocks, wholes):
        block.start()
        whole.start()
    away = core_columns(1 - core[0])
    group = STEPS // 3
    for k in range(0, STEPS, group):
        wait_all(blocks[k : k + group] + wholes[k : k + group])
        rows = pl.ds(k * DEPTH // STEPS, group * DEPTH // STEPS)
        value = product(kept[rows, :], pair[rows, away])
        if k == 0:
            out[...] = value
        else:
            out[...] += value


def second_kernel(
    core, owner_a, owner_b, kept, pair, cotangent, out, pair_a, pair_b, landed_a, landed_b
):
    loads = pair_copies(owner_a[0], cotangent, pair_a, landed_a)
    loads += pair_copies(owner_b[0], cotangent, pair_b, landed_b)
    start_all(loads)
    out[...] = product(kept[...], pair[:, core_columns(core[0])])
    wait_all(loads)


def middle_kernel(
    core, owner, kept, pair_a, pair_b, cotangent, away_a, away_b, out_a, out_b, pair, landed
):
    loads = pair_copies(owner[0], cotangent, pair, landed)
    start_all(loads)
    mine, twin = core_columns(core[0]), core_columns(1 - core[0])
    away_a[...] = product(kept[...], pair_b[:, twin])
    away_b[...] = product(kept[...], pair_a[:, twin])
    out_a[...] = product(kept[...], pair_a[:, mine])
    out_b[...] = product(kept[...], pair_b[:, mine])
    wait_all(loads)


def last_kernel(core, kept, pair, away, out):
    away[...] = product(kept[...], pair[:, core_columns(1 - core[0])])
    out[...] = product(kept[...], pair[:, core_columns(core[0])])


BLOCK = ((ROWS, OWN), F32)
KEPT = ((DEPTH, ROWS), BF16)
PAIR = ((DEPTH, C * OWN), BF16)


def loading_call(kernel, name, limit, in_specs, outs, semaphores, *operands):
    return pl.pallas_call(
        kernel,
        name=name,
        in_specs=in_specs,
        out_specs=[VMEM] * len(outs),
        out_shape=[jax.ShapeDtypeStruct(shape, kind) for shape, kind in outs],
        scratch_shapes=[pltpu.SemaphoreType.DMA((count,)) for count in semaphores],
        compiler_params=pltpu.CompilerParams(vmem_limit_bytes=limit),
        cost_estimate=NO_COST,
    )(*operands)


def lane_sums(block):
    folded = block[:, :LANES] + block[:, LANES:]
    return jnp.sum(folded.T, axis=0, keepdims=True)


def split_rows(core, first_row, halves, mine, away):
    first = core[0] == 0
    for group in range(SHARE):
        at = first_row + group
        a, b = halves[0][group], halves[1][group]
        mine[at : at + 1, :] = jnp.where(first, a, b)
        away[at : at + 1, :] = jnp.where(first, b, a)


def gradient_rows(gradient, half, group):
    at = (half * SHARE + group) * LANES
    return gradient[at : at + LANES, :]


def square_rows_kernel(core, gradient, param, mine, away):
    halves = []
    for half in range(C):
        blocks = [gradient_rows(gradient, half, group) for group in range(SHARE)]
        halves.append([lane_sums(block * block) for block in blocks])
    split_rows(core, 0, halves, mine, away)
    value = param[...]
    total = jnp.full((SHARE, LANES), jnp.sum(value * value))
    mine[SHARE:, :] = total
    away[SHARE:, :] = total


def weighted_rows_kernel(
    core, gradient, col_a, col_b, col_state, mine_in, away_in, new_col, mine, away
):
    col = decay_rate * col_state[...] + (1.0 - decay_rate) * (col_a[...] + col_b[...]) / D
    new_col[...] = col
    inverse = 1.0 / col
    halves = []
    for half in range(C):
        blocks = [gradient_rows(gradient, half, group) for group in range(SHARE)]
        halves.append([lane_sums(block * block * inverse) for block in blocks])
    split_rows(core, 2 * SHARE, halves, mine, away)
    mine[: 2 * SHARE, :] = mine_in[...]
    away[: 2 * SHARE, :] = away_in[...]
    mine[3 * SHARE :, :] = jnp.zeros((SHARE, LANES), F32)
    away[3 * SHARE :, :] = jnp.zeros((SHARE, LANES), F32)


def message_kernel(mine, came, out):
    packed = mine[...] + came[...]
    high = packed.astype(BF16)
    rest = (packed - high.astype(F32)).astype(BF16)
    pieces = [
        high[:SHARE],
        rest[:SHARE],
        high[2 * SHARE : 3 * SHARE],
        high[SHARE : SHARE + 2],
        rest[SHARE : SHARE + 2],
    ]
    message = jnp.concatenate([piece.astype(F32) for piece in pieces], axis=0).astype(BF16)
    for k in range(Y * Z):
        out[k] = message


def reduce_kernel(core, came, row_state, out):
    total = jnp.sum(came[...].astype(F32), axis=0)
    squares = total[:SHARE] + total[SHARE : 2 * SHARE]
    weighted = total[2 * SHARE : 3 * SHARE]
    state = jnp.where(core[0] == 0, row_state[:SHARE, :], row_state[SHARE:, :])
    row = decay_rate * state + (1.0 - decay_rate) * squares / FF
    param_total = total[3 * SHARE : 3 * SHARE + 1] + total[3 * SHARE + 2 : 3 * SHARE + 3]
    out[:SHARE, :] = row
    out[SHARE : SHARE + 1, :] = jnp.full((1, LANES), jnp.sum(weighted / row))
    out[SHARE + 1 : SHARE + 2, :] = jnp.full((1, LANES), jnp.sum(row))
    out[SHARE + 2 :, :] = jnp.broadcast_to(0.5 * param_total, (2, LANES))


def merge_kernel(core, mine, twin, new_row):
    first = core[0] == 0
    a, b = mine[:SHARE, :], twin[:SHARE, :]
    new_row[:SHARE, :] = jnp.where(first, a, b)
    new_row[SHARE:, :] = jnp.where(first, b, a)


def normalise_kernel(gradient, new_row, new_col, update):
    col_factor = lax.rsqrt(new_col[...])
    row_factor = lax.rsqrt(new_row[...])
    for group in range(GROUPS):
        block = gradient[group * LANES : (group + 1) * LANES, :]
        along = jnp.broadcast_to(row_factor[group : group + 1, :], (LANES, LANES)).T
        factor = jnp.concatenate([along, along], axis=1) * col_factor
        update[group * LANES : (group + 1) * LANES, :] = block * factor


def step_kernel(scalars_a, scalars_b, param, update, new_param, stage, sent):
    sums = scalars_a[...] + scalars_b[...]
    entries = D * FF
    row_level = sums[SHARE + 1 : SHARE + 2] / D
    clip = jnp.maximum(1.0, jnp.sqrt(row_level * sums[SHARE : SHARE + 1] / entries))
    scale = jnp.sqrt(sums[SHARE + 2 : SHARE + 3] / entries)
    factor = step_size * scale * jnp.sqrt(row_level) / clip
    factor = jnp.concatenate([factor, factor], axis=1)
    copies = []
    for group in range(GROUPS):
        rows = pl.ds(group * LANES, LANES)
        stage[rows, :] = param[rows, :] - factor * update[rows, :]
        copy = pltpu.make_async_copy(stage.at[rows, :], new_param.at[rows, :], sent.at[group])
        copy.start()
        copies.append(copy)
    wait_all(copies)


def per_device(activations, cotangent, param, row_state, col_state):
    y = lax.axis_index("y")
    c = lax.axis_index("c")
    barrier = lax.optimization_barrier
    way = 2 * c - 1
    hops = [lax.rem(y + Y + hop, Y)[None] for hop in (2, -way, way, 0)]
    *hops, core = barrier((*hops, c[None]))

    def wide(value):
        return value.astype(F32)

    def narrow(value):
        return barrier(value.astype(WIRE))

    def swapped(value, count):
        size = ROWS // count
        parts = [narrow(value[k * size : (k + 1) * size]) for k in range(count)]
        parts = [lax.ppermute(part, "c", swap_core) for part in parts]
        return wide(jnp.concatenate(parts))

    far_away, kept, pair = loading_call(
        first_kernel,
        "first_matmul",
        FIRST_LIMIT,
        [SMEM, SMEM, HBM, HBM],
        [BLOCK, KEPT, PAIR],
        [STEPS, STEPS],
        hops[0],
        core,
        activations,
        cotangent,
    )
    far_came = swapped(far_away, 1)
    far, behind_pair, ahead_pair = loading_call(
        second_kernel,
        "second_matmul",
        SECOND_LIMIT,
        [SMEM, SMEM, SMEM, VMEM, VMEM, HBM],
        [BLOCK, PAIR, PAIR],
        [STEPS, STEPS],
        core,
        hops[1],
        hops[2],
        kept,
        pair,
        cotangent,
    )
    far = narrow(far + far_came)
    far_sent = lax.ppermute(far, ("y", "c"), to_ahead)

    behind_pair, _ = barrier((behind_pair, far))
    behind_away, ahead_away, behind, ahead, own_pair = loading_call(
        middle_kernel,
        "middle_matmul",
        THIRD_LIMIT,
        [SMEM, SMEM, VMEM, VMEM, VMEM, HBM],
        [BLOCK, BLOCK, BLOCK, BLOCK, PAIR],
        [STEPS],
        core,
        hops[3],
        kept,
        behind_pair,
        ahead_pair,
        cotangent,
    )
    behind_came = swapped(behind_away, 4)
    ahead_came = swapped(ahead_away, 4)
    behind = narrow(behind + behind_came)
    behind_sent = lax.ppermute(behind, ("y", "c"), to_behind)
    ahead = narrow(ahead + ahead_came + wide(far_sent))
    ahead_sent = lax.ppermute(ahead, ("y", "c"), to_ahead)

    own_pair, _, _ = barrier((own_pair, behind, ahead))
    own_away, own = call(last_kernel, "last_matmul", [BLOCK, BLOCK], core, kept, own_pair, scalars=1)
    own_came = swapped(own_away, 2)
    gradient = own + own_came + wide(behind_sent) + wide(ahead_sent)

    col_part = jnp.sum(gradient * gradient, axis=0)
    col_part = col_part.reshape(1, OWN)
    col_part = col_part + lax.ppermute(col_part, "x", pair_near)
    col_came = lax.ppermute(col_part, "x", pair_wrap)
    mine, away = call(
        square_rows_kernel, "square_rows", [TILE32, TILE32], core, gradient, param, scalars=1
    )
    new_col, mine, away = call(
        weighted_rows_kernel,
        "weighted_rows",
        [((1, OWN), F32), ((2 * 8, LANES), F32), ((2 * 8, LANES), F32)],
        core,
        gradient,
        col_part,
        col_came,
        col_state.reshape(1, OWN),
        mine,
        away,
        scalars=1,
    )
    came = lax.ppermute(away, "c", swap_core)
    (message,) = call(message_kernel, "message", [((Y * Z, 16, LANES), BF16)], mine, came)
    came = lax.all_to_all(message, ("y", "z"), 0, 0, tiled=True)
    (reduced,) = call(
        reduce_kernel,
        "row_reduce",
        [TILE32],
        core,
        came,
        row_state.reshape(TILE),
        scalars=1,
    )
    twin = lax.ppermute(reduced, "c", swap_core)
    (new_row,) = call(merge_kernel, "merge", [TILE32], core, reduced, twin, scalars=1)
    scalars = reduced + twin
    scalars = scalars + lax.ppermute(scalars, "x", pair_near)
    scalars_came = lax.ppermute(scalars, "x", pair_wrap)
    (update,) = call(
        normalise_kernel, "normalise", [BLOCK], gradient, new_row, new_col
    )
    new_param = pl.pallas_call(
        step_kernel,
        name="step",
        in_specs=[VMEM] * 4,
        out_specs=HBM,
        out_shape=jax.ShapeDtypeStruct((ROWS, OWN), F32),
        scratch_shapes=[pltpu.VMEM((ROWS, OWN), F32), pltpu.SemaphoreType.DMA((GROUPS,))],
        compiler_params=pltpu.CompilerParams(vmem_limit_bytes=LIMIT),
        cost_estimate=NO_COST,
    )(scalars, scalars_came, param, update)
    return (new_param, new_row.reshape(ROWS), new_col.reshape(OWN))


def solution(mesh):
    split = Mesh(mesh.devices.reshape(Y, C, X, Z), ("y", "c", "x", "z"))
    tokens = ("y", "c")
    columns = ("z", "y", "c")
    in_specs = (P(tokens, "x"), P(tokens, "z"), P("x", columns), P("x"), P(columns))
    out_specs = (P("x", columns), P("x"), P(columns))
    return jax.shard_map(
        per_device, mesh=split, in_specs=in_specs, out_specs=out_specs, check_vma=False
    )
```

```python
import jax
import jax.numpy as jnp
from jax import lax
from jax.experimental import pallas as pl
from jax.experimental.pallas import tpu as pltpu
from jax.sharding import Mesh, PartitionSpec as P

D = 4096
FF = 16384
TOKENS = 12288

decay_rate = 0.9
step_size = 0.3

Y, C, X, Z = 4, 2, 4, 8
ROWS = D // X
OWN = FF // (Z * Y * C)
DEPTH = TOKENS // (Y * C)
LANES = 128
GROUPS = ROWS // LANES
SHARE = GROUPS // C
STEPS = 6
WIRE = jnp.float16
F32 = jnp.float32
BF16 = jnp.bfloat16
TILE = (8, LANES)
TILE32 = (TILE, F32)

swap_core = [(0, 1), (1, 0)]
turn = (-1, 1)
to_ahead = [(i * C + k, (i + turn[k]) % Y * C + k) for i in range(Y) for k in range(C)]
to_behind = [(i * C + k, (i - turn[k]) % Y * C + k) for i in range(Y) for k in range(C)]
pair_near = [(i, i ^ 1) for i in range(X)]
pair_wrap = [(i, X - 1 - i) for i in range(X)]
pair_cross = [(i, (i + 2) % X) for i in range(X)]

VMEM = pl.BlockSpec(memory_space=pltpu.VMEM)
SMEM = pl.BlockSpec(memory_space=pltpu.SMEM)
HBM = pl.BlockSpec(memory_space=pltpu.HBM)
LIMIT = 14 * 2**20
FIRST_LIMIT = 48 * 2**20
SECOND_LIMIT = 43 * 2**20
LAST_LIMIT = 43 * 2**20
NO_COST = pl.CostEstimate(flops=1, bytes_accessed=1, transcendentals=0)


def call(kernel, name, outs, *operands, scalars=0):
    return pl.pallas_call(
        kernel,
        name=name,
        in_specs=[SMEM] * scalars + [VMEM] * (len(operands) - scalars),
        out_specs=[VMEM] * len(outs),
        out_shape=[jax.ShapeDtypeStruct(shape, kind) for shape, kind in outs],
        compiler_params=pltpu.CompilerParams(vmem_limit_bytes=LIMIT),
        cost_estimate=NO_COST,
    )(*operands)


def load_rows(k):
    return pl.ds(k * DEPTH // STEPS, DEPTH // STEPS)


def column_copies(place, width, cotangent, block, landed):
    columns = pl.ds(pl.multiple_of(place * width, width), width)
    return [
        pltpu.make_async_copy(
            cotangent.at[load_rows(k), columns], block.at[load_rows(k), :], landed.at[k]
        )
        for k in range(STEPS)
    ]


def start_all(copies):
    for copy in copies:
        copy.start()


def wait_all(copies):
    for copy in copies:
        copy.wait()


def product(left, right):
    return lax.dot_general(left, right, (((0,), (0,)), ((), ())), preferred_element_type=F32)


def core_columns(core):
    return pl.ds(pl.multiple_of(core * OWN, OWN), OWN)


def first_kernel(owner, core, activations, cotangent, out, kept, pair, arrived, landed):
    blocks = column_copies(owner[0], C * OWN, cotangent, pair, landed)
    wholes = [
        pltpu.make_async_copy(
            activations.at[load_rows(k), :], kept.at[load_rows(k), :], arrived.at[k]
        )
        for k in range(STEPS)
    ]
    for block, whole in zip(blocks, wholes):
        block.start()
        whole.start()
    away = core_columns(1 - core[0])
    group = STEPS // 3
    for k in range(0, STEPS, group):
        wait_all(blocks[k : k + group] + wholes[k : k + group])
        rows = pl.ds(k * DEPTH // STEPS, group * DEPTH // STEPS)
        value = product(kept[rows, :], pair[rows, away])
        if k == 0:
            out[...] = value
        else:
            out[...] += value


def block_loads(owner_a, owner_b, core, cotangent, block_a, block_b, landed_a, landed_b):
    loads = column_copies(owner_a[0] * C + core, OWN, cotangent, block_a, landed_a)
    return loads + column_copies(owner_b[0] * C + core, OWN, cotangent, block_b, landed_b)


def second_kernel(
    core, behind, ahead, kept, pair, cotangent, out, a, b, mine_a, mine_b, *landed
):
    loads = block_loads(ahead, behind, 1 - core[0], cotangent, a, b, *landed[:2])
    loads += block_loads(behind, ahead, core[0], cotangent, mine_a, mine_b, *landed[2:])
    start_all(loads)
    out[...] = product(kept[...], pair[:, core_columns(core[0])])
    wait_all(loads)


def two_kernel(kept, a, b, out_a, out_b):
    out_a[...] = product(kept[...], a[...])
    out_b[...] = product(kept[...], b[...])


def last_kernel(core, owner, kept, cotangent, away, out, pair, landed):
    loads = column_copies(owner[0], C * OWN, cotangent, pair, landed)
    start_all(loads)
    wait_all(loads)
    away[...] = product(kept[...], pair[:, core_columns(1 - core[0])])
    out[...] = product(kept[...], pair[:, core_columns(core[0])])


BLOCK = ((ROWS, OWN), F32)
KEPT = ((DEPTH, ROWS), BF16)
PAIR = ((DEPTH, C * OWN), BF16)
HALF = ((DEPTH, OWN), BF16)


def loading_call(kernel, name, limit, in_specs, outs, semaphores, *operands):
    return pl.pallas_call(
        kernel,
        name=name,
        in_specs=in_specs,
        out_specs=[VMEM] * len(outs),
        out_shape=[jax.ShapeDtypeStruct(shape, kind) for shape, kind in outs],
        scratch_shapes=[pltpu.SemaphoreType.DMA((count,)) for count in semaphores],
        compiler_params=pltpu.CompilerParams(vmem_limit_bytes=limit),
        cost_estimate=NO_COST,
    )(*operands)


def lane_sums(block):
    folded = block[:, :LANES] + block[:, LANES:]
    return jnp.sum(folded.T, axis=0, keepdims=True)


def split_rows(core, first_row, halves, mine, away):
    first = core[0] == 0
    for group in range(SHARE):
        at = first_row + group
        a, b = halves[0][group], halves[1][group]
        mine[at : at + 1, :] = jnp.where(first, a, b)
        away[at : at + 1, :] = jnp.where(first, b, a)


def gradient_rows(gradient, half, group):
    at = (half * SHARE + group) * LANES
    return gradient[at : at + LANES, :]


def square_rows_kernel(core, gradient, param, mine, away):
    halves = []
    for half in range(C):
        blocks = [gradient_rows(gradient, half, group) for group in range(SHARE)]
        halves.append([lane_sums(block * block) for block in blocks])
    split_rows(core, 0, halves, mine, away)
    value = param[...]
    total = jnp.full((SHARE, LANES), jnp.sum(value * value))
    mine[SHARE:, :] = total
    away[SHARE:, :] = total


def column_state(col_a, col_b, col_state):
    return decay_rate * col_state[...] + (1.0 - decay_rate) * (col_a[...] + col_b[...]) / D


def weighted_rows_kernel(core, gradient, col_a, col_b, col_state, mine_in, away_in, mine, away):
    inverse = 1.0 / column_state(col_a, col_b, col_state)
    halves = []
    for half in range(C):
        blocks = [gradient_rows(gradient, half, group) for group in range(SHARE)]
        halves.append([lane_sums(block * block * inverse) for block in blocks])
    split_rows(core, 2 * SHARE, halves, mine, away)
    mine[: 2 * SHARE, :] = mine_in[...]
    away[: 2 * SHARE, :] = away_in[...]
    mine[3 * SHARE :, :] = jnp.zeros((SHARE, LANES), F32)
    away[3 * SHARE :, :] = jnp.zeros((SHARE, LANES), F32)


def message_kernel(mine, came, out):
    packed = mine[...] + came[...]
    high = packed.astype(BF16)
    rest = (packed - high.astype(F32)).astype(BF16)
    pieces = [
        high[:SHARE],
        rest[:SHARE],
        high[2 * SHARE : 3 * SHARE],
        high[SHARE : SHARE + 2],
        rest[SHARE : SHARE + 2],
    ]
    message = jnp.concatenate([piece.astype(F32) for piece in pieces], axis=0).astype(BF16)
    for k in range(Y * Z):
        out[k] = message


def reduce_kernel(core, came, row_state, out):
    total = jnp.sum(came[...].astype(F32), axis=0)
    squares = total[:SHARE] + total[SHARE : 2 * SHARE]
    weighted = total[2 * SHARE : 3 * SHARE]
    state = jnp.where(core[0] == 0, row_state[:SHARE, :], row_state[SHARE:, :])
    row = decay_rate * state + (1.0 - decay_rate) * squares / FF
    param_total = total[3 * SHARE : 3 * SHARE + 1] + total[3 * SHARE + 2 : 3 * SHARE + 3]
    out[:SHARE, :] = row
    out[SHARE : SHARE + 1, :] = jnp.full((1, LANES), jnp.sum(weighted / row))
    out[SHARE + 1 : SHARE + 2, :] = jnp.full((1, LANES), jnp.sum(row))
    out[SHARE + 2 :, :] = jnp.broadcast_to(0.5 * param_total, (2, LANES))


def whole_rows(core, mine, twin):
    first = core[0] == 0
    a, b = mine[:SHARE, :], twin[:SHARE, :]
    return jnp.concatenate([jnp.where(first, a, b), jnp.where(first, b, a)], axis=0)


def normalise_kernel(
    core, gradient, mine, twin, col_a, col_b, col_state, update, new_row, new_col
):
    col = column_state(col_a, col_b, col_state)
    row = whole_rows(core, mine, twin)
    new_col[...] = col
    new_row[...] = row
    col_factor = lax.rsqrt(col)
    row_factor = lax.rsqrt(row)
    for group in range(GROUPS):
        block = gradient[group * LANES : (group + 1) * LANES, :]
        along = jnp.broadcast_to(row_factor[group : group + 1, :], (LANES, LANES)).T
        factor = jnp.concatenate([along, along], axis=1) * col_factor
        update[group * LANES : (group + 1) * LANES, :] = block * factor


def step_kernel(scalars_a, scalars_b, param, update, new_param, stage, sent):
    sums = scalars_a[...] + scalars_b[...]
    entries = D * FF
    row_level = sums[SHARE + 1 : SHARE + 2] / D
    clip = jnp.maximum(1.0, jnp.sqrt(row_level * sums[SHARE : SHARE + 1] / entries))
    scale = jnp.sqrt(sums[SHARE + 2 : SHARE + 3] / entries)
    factor = step_size * scale * jnp.sqrt(row_level) / clip
    factor = jnp.concatenate([factor, factor], axis=1)
    copies = []
    for group in range(GROUPS):
        rows = pl.ds(group * LANES, LANES)
        stage[rows, :] = param[rows, :] - factor * update[rows, :]
        copy = pltpu.make_async_copy(stage.at[rows, :], new_param.at[rows, :], sent.at[group])
        copy.start()
        copies.append(copy)
    wait_all(copies)


def per_device(activations, cotangent, param, row_state, col_state):
    y = lax.axis_index("y")
    c = lax.axis_index("c")
    barrier = lax.optimization_barrier
    way = 2 * c - 1
    hops = [lax.rem(y + Y + hop, Y)[None] for hop in (2, -way, way, 0)]
    *hops, core = barrier((*hops, c[None]))

    def wide(value):
        return value.astype(F32)

    def narrow(value):
        return barrier(value.astype(WIRE))

    def swapped(value, count):
        cuts = [ROWS * k // count // 16 * 16 for k in range(count + 1)]
        parts = [narrow(value[a:b]) for a, b in zip(cuts, cuts[1:])]
        parts = [lax.ppermute(part, "c", swap_core) for part in parts]
        return wide(jnp.concatenate(parts))

    far_away, kept, pair = loading_call(
        first_kernel,
        "first_matmul",
        FIRST_LIMIT,
        [SMEM, SMEM, HBM, HBM],
        [BLOCK, KEPT, PAIR],
        [STEPS, STEPS],
        hops[0],
        core,
        activations,
        cotangent,
    )
    far_came = swapped(far_away, 1)
    far, away_a, away_b, mine_a, mine_b = loading_call(
        second_kernel,
        "second_matmul",
        SECOND_LIMIT,
        [SMEM, SMEM, SMEM, VMEM, VMEM, HBM],
        [BLOCK, HALF, HALF, HALF, HALF],
        [STEPS] * 4,
        core,
        hops[1],
        hops[2],
        kept,
        pair,
        cotangent,
    )
    far = narrow(far + far_came)
    far_sent = lax.ppermute(far, ("y", "c"), to_ahead)

    away_a, _ = barrier((away_a, far))
    behind_away, ahead_away = call(
        two_kernel, "third_matmul", [BLOCK, BLOCK], kept, away_a, away_b
    )
    behind_came = swapped(behind_away, 3)
    ahead_came = swapped(ahead_away, 2)
    mine_a, _, _ = barrier((mine_a, behind_away, ahead_away))
    behind, ahead = call(two_kernel, "fourth_matmul", [BLOCK, BLOCK], kept, mine_a, mine_b)
    behind = narrow(behind + behind_came)
    behind_sent = lax.ppermute(behind, ("y", "c"), to_behind)
    ahead, _ = barrier((ahead, behind))
    ahead = narrow(ahead + ahead_came + wide(far_sent))
    ahead_sent = lax.ppermute(ahead, ("y", "c"), to_ahead)

    kept, _ = barrier((kept, ahead))
    own_away, own = pl.pallas_call(
        last_kernel,
        name="last_matmul",
        in_specs=[SMEM, SMEM, VMEM, HBM],
        out_specs=[VMEM, VMEM],
        out_shape=[jax.ShapeDtypeStruct(*BLOCK)] * 2,
        scratch_shapes=[pltpu.VMEM(*PAIR), pltpu.SemaphoreType.DMA((STEPS,))],
        compiler_params=pltpu.CompilerParams(vmem_limit_bytes=LAST_LIMIT),
        cost_estimate=NO_COST,
    )(core, hops[3], kept, cotangent)
    own_came = swapped(own_away, 2)
    gradient = own + own_came + wide(behind_sent) + wide(ahead_sent)

    col_part = jnp.sum(gradient * gradient, axis=0)
    col_part = col_part.reshape(1, OWN)
    col_came = (
        lax.ppermute(col_part, "x", pair_cross)
        + lax.ppermute(col_part, "x", pair_near)
        + lax.ppermute(col_part, "x", pair_wrap)
    )
    mine, away = call(
        square_rows_kernel, "square_rows", [TILE32, TILE32], core, gradient, param, scalars=1
    )
    columns = (col_part, col_came, col_state.reshape(1, OWN))
    mine, away = call(
        weighted_rows_kernel,
        "weighted_rows",
        [((2 * 8, LANES), F32), ((2 * 8, LANES), F32)],
        core,
        gradient,
        *columns,
        mine,
        away,
        scalars=1,
    )
    came = lax.ppermute(away, "c", swap_core)
    (message,) = call(message_kernel, "message", [((Y * Z, 16, LANES), BF16)], mine, came)
    came = lax.all_to_all(message, ("y", "z"), 0, 0, tiled=True)
    (reduced,) = call(
        reduce_kernel,
        "row_reduce",
        [TILE32],
        core,
        came,
        row_state.reshape(TILE),
        scalars=1,
    )
    twin = lax.ppermute(reduced, "c", swap_core)
    scalars = reduced + twin
    scalars_came = (
        lax.ppermute(scalars, "x", pair_cross)
        + lax.ppermute(scalars, "x", pair_near)
        + lax.ppermute(scalars, "x", pair_wrap)
    )
    update, new_row, new_col = call(
        normalise_kernel,
        "normalise",
        [BLOCK, TILE32, ((1, OWN), F32)],
        core,
        gradient,
        reduced,
        twin,
        *columns,
        scalars=1,
    )
    new_param = pl.pallas_call(
        step_kernel,
        name="step",
        in_specs=[VMEM] * 4,
        out_specs=HBM,
        out_shape=jax.ShapeDtypeStruct((ROWS, OWN), F32),
        scratch_shapes=[pltpu.VMEM((ROWS, OWN), F32), pltpu.SemaphoreType.DMA((GROUPS,))],
        compiler_params=pltpu.CompilerParams(vmem_limit_bytes=LIMIT),
        cost_estimate=NO_COST,
    )(scalars, scalars_came, param, update)
    return (new_param, new_row.reshape(ROWS), new_col.reshape(OWN))


def solution(mesh):
    split = Mesh(mesh.devices.reshape(Y, C, X, Z), ("y", "c", "x", "z"))
    tokens = ("y", "c")
    columns = ("z", "y", "c")
    in_specs = (P(tokens, "x"), P(tokens, "z"), P("x", columns), P("x"), P(columns))
    out_specs = (P("x", columns), P("x"), P(columns))
    return jax.shard_map(
        per_device, mesh=split, in_specs=in_specs, out_specs=out_specs, check_vma=False
    )
```

```python
import jax
import jax.numpy as jnp
from jax import lax
from jax.experimental import pallas as pl
from jax.experimental.pallas import tpu as pltpu
from jax.sharding import Mesh, PartitionSpec as P

D = 4096
FF = 16384
TOKENS = 12288

decay_rate = 0.9
step_size = 0.3

Y, C, X, Z = 4, 2, 4, 8
ROWS = D // X
OWN = FF // (Z * Y * C)
DEPTH = TOKENS // (Y * C)
LANES = 128
GROUPS = ROWS // LANES
SHARE = GROUPS // C
STEPS = 6
WIRE = jnp.float16
F32 = jnp.float32
BF16 = jnp.bfloat16
TILE = (8, LANES)
TILE32 = (TILE, F32)

swap_core = [(0, 1), (1, 0)]
turn = (-1, 1)
to_ahead = [(i * C + k, (i + turn[k]) % Y * C + k) for i in range(Y) for k in range(C)]
to_behind = [(i * C + k, (i - turn[k]) % Y * C + k) for i in range(Y) for k in range(C)]
pair_near = [(i, i ^ 1) for i in range(X)]
pair_wrap = [(i, X - 1 - i) for i in range(X)]
pair_cross = [(i, (i + 2) % X) for i in range(X)]

VMEM = pl.BlockSpec(memory_space=pltpu.VMEM)
SMEM = pl.BlockSpec(memory_space=pltpu.SMEM)
HBM = pl.BlockSpec(memory_space=pltpu.HBM)
LIMIT = 14 * 2**20
FIRST_LIMIT = 48 * 2**20
SECOND_LIMIT = 43 * 2**20
LAST_LIMIT = 43 * 2**20
MIDDLE_LIMIT = 42 * 2**20
NO_COST = pl.CostEstimate(flops=1, bytes_accessed=1, transcendentals=0)


def call(kernel, name, outs, *operands, scalars=0):
    return pl.pallas_call(
        kernel,
        name=name,
        in_specs=[SMEM] * scalars + [VMEM] * (len(operands) - scalars),
        out_specs=[VMEM] * len(outs),
        out_shape=[jax.ShapeDtypeStruct(shape, kind) for shape, kind in outs],
        compiler_params=pltpu.CompilerParams(vmem_limit_bytes=LIMIT),
        cost_estimate=NO_COST,
    )(*operands)


def load_rows(k):
    return pl.ds(k * DEPTH // STEPS, DEPTH // STEPS)


def column_copies(place, width, cotangent, block, landed):
    columns = pl.ds(pl.multiple_of(place * width, width), width)
    return [
        pltpu.make_async_copy(
            cotangent.at[load_rows(k), columns], block.at[load_rows(k), :], landed.at[k]
        )
        for k in range(STEPS)
    ]


def start_all(copies):
    for copy in copies:
        copy.start()


def wait_all(copies):
    for copy in copies:
        copy.wait()


def product(left, right):
    return lax.dot_general(left, right, (((0,), (0,)), ((), ())), preferred_element_type=F32)


def core_columns(core):
    return pl.ds(pl.multiple_of(core * OWN, OWN), OWN)


def first_kernel(owner, core, activations, cotangent, out, kept, pair, arrived, landed):
    blocks = column_copies(owner[0], C * OWN, cotangent, pair, landed)
    wholes = [
        pltpu.make_async_copy(
            activations.at[load_rows(k), :], kept.at[load_rows(k), :], arrived.at[k]
        )
        for k in range(STEPS)
    ]
    for block, whole in zip(blocks, wholes):
        block.start()
        whole.start()
    away = core_columns(1 - core[0])
    group = STEPS // 3
    for k in range(0, STEPS, group):
        wait_all(blocks[k : k + group] + wholes[k : k + group])
        rows = pl.ds(k * DEPTH // STEPS, group * DEPTH // STEPS)
        value = product(kept[rows, :], pair[rows, away])
        if k == 0:
            out[...] = value
        else:
            out[...] += value


def block_loads(owner_a, owner_b, core, cotangent, block_a, block_b, landed_a, landed_b):
    loads = column_copies(owner_a[0] * C + core, OWN, cotangent, block_a, landed_a)
    return loads + column_copies(owner_b[0] * C + core, OWN, cotangent, block_b, landed_b)


def second_kernel(
    core, behind, ahead, kept, pair, cotangent, out, a, b, mine, landed_a, landed_b, landed
):
    loads = block_loads(ahead, behind, 1 - core[0], cotangent, a, b, landed_a, landed_b)
    loads += column_copies(ahead[0] * C + core[0], OWN, cotangent, mine, landed)
    start_all(loads)
    out[...] = product(kept[...], pair[:, core_columns(core[0])])
    wait_all(loads)


def third_kernel(core, behind, kept, a, b, cotangent, out_a, out_b, mine, landed):
    loads = column_copies(behind[0] * C + core[0], OWN, cotangent, mine, landed)
    start_all(loads)
    out_a[...] = product(kept[...], a[...])
    out_b[...] = product(kept[...], b[...])
    wait_all(loads)


def fourth_kernel(kept, a, b, out_a, out_b):
    out_a[...] = product(kept[...], a[...])
    out_b[...] = product(kept[...], b[...])


def last_kernel(core, owner, kept, cotangent, away, out, pair, landed):
    loads = column_copies(owner[0], C * OWN, cotangent, pair, landed)
    start_all(loads)
    wait_all(loads)
    away[...] = product(kept[...], pair[:, core_columns(1 - core[0])])
    out[...] = product(kept[...], pair[:, core_columns(core[0])])


BLOCK = ((ROWS, OWN), F32)
KEPT = ((DEPTH, ROWS), BF16)
PAIR = ((DEPTH, C * OWN), BF16)
HALF = ((DEPTH, OWN), BF16)


def loading_call(kernel, name, limit, in_specs, outs, semaphores, *operands):
    return pl.pallas_call(
        kernel,
        name=name,
        in_specs=in_specs,
        out_specs=[VMEM] * len(outs),
        out_shape=[jax.ShapeDtypeStruct(shape, kind) for shape, kind in outs],
        scratch_shapes=[pltpu.SemaphoreType.DMA((count,)) for count in semaphores],
        compiler_params=pltpu.CompilerParams(vmem_limit_bytes=limit),
        cost_estimate=NO_COST,
    )(*operands)


def lane_sums(block):
    folded = block[:, :LANES] + block[:, LANES:]
    return jnp.sum(folded.T, axis=0, keepdims=True)


def split_rows(core, first_row, halves, mine, away):
    first = core[0] == 0
    for group in range(SHARE):
        at = first_row + group
        a, b = halves[0][group], halves[1][group]
        mine[at : at + 1, :] = jnp.where(first, a, b)
        away[at : at + 1, :] = jnp.where(first, b, a)


def gradient_rows(gradient, half, group):
    at = (half * SHARE + group) * LANES
    return gradient[at : at + LANES, :]


def square_rows_kernel(core, gradient, param, mine, away):
    halves = []
    for half in range(C):
        blocks = [gradient_rows(gradient, half, group) for group in range(SHARE)]
        halves.append([lane_sums(block * block) for block in blocks])
    split_rows(core, 0, halves, mine, away)
    value = param[...]
    total = jnp.full((SHARE, LANES), jnp.sum(value * value))
    mine[SHARE:, :] = total
    away[SHARE:, :] = total


def column_state(col_a, col_b, col_state):
    return decay_rate * col_state[...] + (1.0 - decay_rate) * (col_a[...] + col_b[...]) / D


def weighted_rows_kernel(core, gradient, col_a, col_b, col_state, mine_in, away_in, mine, away):
    inverse = 1.0 / column_state(col_a, col_b, col_state)
    halves = []
    for half in range(C):
        blocks = [gradient_rows(gradient, half, group) for group in range(SHARE)]
        halves.append([lane_sums(block * block * inverse) for block in blocks])
    split_rows(core, 2 * SHARE, halves, mine, away)
    mine[: 2 * SHARE, :] = mine_in[...]
    away[: 2 * SHARE, :] = away_in[...]
    mine[3 * SHARE :, :] = jnp.zeros((SHARE, LANES), F32)
    away[3 * SHARE :, :] = jnp.zeros((SHARE, LANES), F32)


def message_kernel(mine, came, out):
    packed = mine[...] + came[...]
    high = packed.astype(BF16)
    rest = (packed - high.astype(F32)).astype(BF16)
    pieces = [
        high[:SHARE],
        rest[:SHARE],
        high[2 * SHARE : 3 * SHARE],
        high[SHARE : SHARE + 2],
        rest[SHARE : SHARE + 2],
    ]
    message = jnp.concatenate([piece.astype(F32) for piece in pieces], axis=0).astype(BF16)
    for k in range(Y * Z):
        out[k] = message


def reduce_kernel(core, came, row_state, out):
    total = jnp.sum(came[...].astype(F32), axis=0)
    squares = total[:SHARE] + total[SHARE : 2 * SHARE]
    weighted = total[2 * SHARE : 3 * SHARE]
    state = jnp.where(core[0] == 0, row_state[:SHARE, :], row_state[SHARE:, :])
    row = decay_rate * state + (1.0 - decay_rate) * squares / FF
    param_total = total[3 * SHARE : 3 * SHARE + 1] + total[3 * SHARE + 2 : 3 * SHARE + 3]
    out[:SHARE, :] = row
    out[SHARE : SHARE + 1, :] = jnp.full((1, LANES), jnp.sum(weighted / row))
    out[SHARE + 1 : SHARE + 2, :] = jnp.full((1, LANES), jnp.sum(row))
    out[SHARE + 2 :, :] = jnp.broadcast_to(0.5 * param_total, (2, LANES))


def whole_rows(core, mine, twin):
    first = core[0] == 0
    a, b = mine[:SHARE, :], twin[:SHARE, :]
    return jnp.concatenate([jnp.where(first, a, b), jnp.where(first, b, a)], axis=0)


def normalise_kernel(
    core, gradient, mine, twin, col_a, col_b, col_state, update, new_row, new_col
):
    col = column_state(col_a, col_b, col_state)
    row = whole_rows(core, mine, twin)
    new_col[...] = col
    new_row[...] = row
    col_factor = lax.rsqrt(col)
    row_factor = lax.rsqrt(row)
    for group in range(GROUPS):
        block = gradient[group * LANES : (group + 1) * LANES, :]
        along = jnp.broadcast_to(row_factor[group : group + 1, :], (LANES, LANES)).T
        factor = jnp.concatenate([along, along], axis=1) * col_factor
        update[group * LANES : (group + 1) * LANES, :] = block * factor


def step_kernel(scalars_a, scalars_b, param, update, new_param, stage, sent):
    sums = scalars_a[...] + scalars_b[...]
    entries = D * FF
    row_level = sums[SHARE + 1 : SHARE + 2] / D
    clip = jnp.maximum(1.0, jnp.sqrt(row_level * sums[SHARE : SHARE + 1] / entries))
    scale = jnp.sqrt(sums[SHARE + 2 : SHARE + 3] / entries)
    factor = step_size * scale * jnp.sqrt(row_level) / clip
    factor = jnp.concatenate([factor, factor], axis=1)
    copies = []
    for group in range(GROUPS):
        rows = pl.ds(group * LANES, LANES)
        stage[rows, :] = param[rows, :] - factor * update[rows, :]
        copy = pltpu.make_async_copy(stage.at[rows, :], new_param.at[rows, :], sent.at[group])
        copy.start()
        copies.append(copy)
    wait_all(copies)


def per_device(activations, cotangent, param, row_state, col_state):
    y = lax.axis_index("y")
    c = lax.axis_index("c")
    barrier = lax.optimization_barrier
    way = 2 * c - 1
    hops = [lax.rem(y + Y + hop, Y)[None] for hop in (2, -way, way, 0)]
    *hops, core = barrier((*hops, c[None]))

    def wide(value):
        return value.astype(F32)

    def narrow(value):
        return barrier(value.astype(WIRE))

    def swapped(value, count):
        cuts = [ROWS * k // count // 16 * 16 for k in range(count + 1)]
        parts = [narrow(value[a:b]) for a, b in zip(cuts, cuts[1:])]
        parts = [lax.ppermute(part, "c", swap_core) for part in parts]
        return wide(jnp.concatenate(parts))

    far_away, kept, pair = loading_call(
        first_kernel,
        "first_matmul",
        FIRST_LIMIT,
        [SMEM, SMEM, HBM, HBM],
        [BLOCK, KEPT, PAIR],
        [STEPS, STEPS],
        hops[0],
        core,
        activations,
        cotangent,
    )
    far_came = swapped(far_away, 1)
    far, away_a, away_b, mine_b = loading_call(
        second_kernel,
        "second_matmul",
        SECOND_LIMIT,
        [SMEM, SMEM, SMEM, VMEM, VMEM, HBM],
        [BLOCK, HALF, HALF, HALF],
        [STEPS] * 3,
        core,
        hops[1],
        hops[2],
        kept,
        pair,
        cotangent,
    )
    far = narrow(far + far_came)
    far_sent = lax.ppermute(far, ("y", "c"), to_ahead)

    away_a, _ = barrier((away_a, far))
    behind_away, ahead_away, mine_a = loading_call(
        third_kernel,
        "third_matmul",
        MIDDLE_LIMIT,
        [SMEM, SMEM, VMEM, VMEM, VMEM, HBM],
        [BLOCK, BLOCK, HALF],
        [STEPS],
        core,
        hops[1],
        kept,
        away_a,
        away_b,
        cotangent,
    )
    behind_came = swapped(behind_away, 3)
    ahead_came = swapped(ahead_away, 1)
    behind, ahead = call(fourth_kernel, "fourth_matmul", [BLOCK, BLOCK], kept, mine_a, mine_b)
    behind = narrow(behind + behind_came)
    behind_sent = lax.ppermute(behind, ("y", "c"), to_behind)
    ahead, _ = barrier((ahead, behind))
    ahead = narrow(ahead + ahead_came + wide(far_sent))
    ahead_sent = lax.ppermute(ahead, ("y", "c"), to_ahead)

    kept, _ = barrier((kept, ahead))
    own_away, own = pl.pallas_call(
        last_kernel,
        name="last_matmul",
        in_specs=[SMEM, SMEM, VMEM, HBM],
        out_specs=[VMEM, VMEM],
        out_shape=[jax.ShapeDtypeStruct(*BLOCK)] * 2,
        scratch_shapes=[pltpu.VMEM(*PAIR), pltpu.SemaphoreType.DMA((STEPS,))],
        compiler_params=pltpu.CompilerParams(vmem_limit_bytes=LAST_LIMIT),
        cost_estimate=NO_COST,
    )(core, hops[3], kept, cotangent)
    own_came = swapped(own_away, 2)
    gradient = own + own_came + wide(behind_sent) + wide(ahead_sent)

    col_part = jnp.sum(gradient * gradient, axis=0)
    col_part = col_part.reshape(1, OWN)
    col_came = (
        lax.ppermute(col_part, "x", pair_near)
        + lax.ppermute(col_part, "x", pair_wrap)
        + lax.ppermute(col_part, "x", pair_cross)
    )
    mine, away = call(
        square_rows_kernel, "square_rows", [TILE32, TILE32], core, gradient, param, scalars=1
    )
    columns = (col_part, col_came, col_state.reshape(1, OWN))
    mine, away = call(
        weighted_rows_kernel,
        "weighted_rows",
        [((2 * 8, LANES), F32), ((2 * 8, LANES), F32)],
        core,
        gradient,
        *columns,
        mine,
        away,
        scalars=1,
    )
    came = lax.ppermute(away, "c", swap_core)
    (message,) = call(message_kernel, "message", [((Y * Z, 16, LANES), BF16)], mine, came)
    came = lax.all_to_all(message, ("y", "z"), 0, 0, tiled=True)
    (reduced,) = call(
        reduce_kernel,
        "row_reduce",
        [TILE32],
        core,
        came,
        row_state.reshape(TILE),
        scalars=1,
    )
    twin = lax.ppermute(reduced, "c", swap_core)
    scalars = reduced + twin
    scalars_came = (
        lax.ppermute(scalars, "x", pair_near)
        + lax.ppermute(scalars, "x", pair_wrap)
        + lax.ppermute(scalars, "x", pair_cross)
    )
    update, new_row, new_col = call(
        normalise_kernel,
        "normalise",
        [BLOCK, TILE32, ((1, OWN), F32)],
        core,
        gradient,
        reduced,
        twin,
        *columns,
        scalars=1,
    )
    new_param = pl.pallas_call(
        step_kernel,
        name="step",
        in_specs=[VMEM] * 4,
        out_specs=HBM,
        out_shape=jax.ShapeDtypeStruct((ROWS, OWN), F32),
        scratch_shapes=[pltpu.VMEM((ROWS, OWN), F32), pltpu.SemaphoreType.DMA((GROUPS,))],
        compiler_params=pltpu.CompilerParams(vmem_limit_bytes=LIMIT),
        cost_estimate=NO_COST,
    )(scalars, scalars_came, param, update)
    return (new_param, new_row.reshape(ROWS), new_col.reshape(OWN))


def solution(mesh):
    split = Mesh(mesh.devices.reshape(Y, C, X, Z), ("y", "c", "x", "z"))
    tokens = ("y", "c")
    columns = ("z", "y", "c")
    in_specs = (P(tokens, "x"), P(tokens, "z"), P("x", columns), P("x"), P(columns))
    out_specs = (P("x", columns), P("x"), P(columns))
    return jax.shard_map(
        per_device, mesh=split, in_specs=in_specs, out_specs=out_specs, check_vma=False
    )
```

```python
import jax
import jax.numpy as jnp
from jax import lax
from jax.experimental import pallas as pl
from jax.experimental.pallas import tpu as pltpu
from jax.sharding import Mesh, PartitionSpec as P

D = 4096
FF = 16384
TOKENS = 12288

decay_rate = 0.9
step_size = 0.3

Y, C, X, Z = 4, 2, 4, 8
ROWS = D // X
OWN = FF // (Z * Y * C)
DEPTH = TOKENS // (Y * C)
LANES = 128
GROUPS = ROWS // LANES
SHARE = GROUPS // C
STEPS = 6
WIRE = jnp.float16
F32 = jnp.float32
BF16 = jnp.bfloat16
TILE = (8, LANES)
TILE32 = (TILE, F32)

swap_core = [(0, 1), (1, 0)]
turn = (-1, 1)
to_ahead = [(i * C + k, (i + turn[k]) % Y * C + k) for i in range(Y) for k in range(C)]
to_behind = [(i * C + k, (i - turn[k]) % Y * C + k) for i in range(Y) for k in range(C)]
pair_near = [(i, i ^ 1) for i in range(X)]
pair_wrap = [(i, X - 1 - i) for i in range(X)]
pair_cross = [(i, (i + 2) % X) for i in range(X)]

VMEM = pl.BlockSpec(memory_space=pltpu.VMEM)
SMEM = pl.BlockSpec(memory_space=pltpu.SMEM)
HBM = pl.BlockSpec(memory_space=pltpu.HBM)
LIMIT = 14 * 2**20
FIRST_LIMIT = 48 * 2**20
SECOND_LIMIT = 43 * 2**20
LAST_LIMIT = 43 * 2**20
MIDDLE_LIMIT = 42 * 2**20
NO_COST = pl.CostEstimate(flops=1, bytes_accessed=1, transcendentals=0)


def call(kernel, name, outs, *operands, scalars=0):
    return pl.pallas_call(
        kernel,
        name=name,
        in_specs=[SMEM] * scalars + [VMEM] * (len(operands) - scalars),
        out_specs=[VMEM] * len(outs),
        out_shape=[jax.ShapeDtypeStruct(shape, kind) for shape, kind in outs],
        compiler_params=pltpu.CompilerParams(vmem_limit_bytes=LIMIT),
        cost_estimate=NO_COST,
    )(*operands)


def load_rows(k):
    return pl.ds(k * DEPTH // STEPS, DEPTH // STEPS)


def column_copies(place, width, cotangent, block, landed):
    columns = pl.ds(pl.multiple_of(place * width, width), width)
    return [
        pltpu.make_async_copy(
            cotangent.at[load_rows(k), columns], block.at[load_rows(k), :], landed.at[k]
        )
        for k in range(STEPS)
    ]


def start_all(copies):
    for copy in copies:
        copy.start()


def wait_all(copies):
    for copy in copies:
        copy.wait()


def product(left, right):
    return lax.dot_general(left, right, (((0,), (0,)), ((), ())), preferred_element_type=F32)


def core_columns(core):
    return pl.ds(pl.multiple_of(core * OWN, OWN), OWN)


def first_kernel(owner, core, activations, cotangent, out, kept, pair, arrived, landed):
    blocks = column_copies(owner[0], C * OWN, cotangent, pair, landed)
    wholes = [
        pltpu.make_async_copy(
            activations.at[load_rows(k), :], kept.at[load_rows(k), :], arrived.at[k]
        )
        for k in range(STEPS)
    ]
    for block, whole in zip(blocks, wholes):
        block.start()
        whole.start()
    away = core_columns(1 - core[0])
    group = STEPS // 3
    for k in range(0, STEPS, group):
        wait_all(blocks[k : k + group] + wholes[k : k + group])
        rows = pl.ds(k * DEPTH // STEPS, group * DEPTH // STEPS)
        value = product(kept[rows, :], pair[rows, away])
        if k == 0:
            out[...] = value
        else:
            out[...] += value


def block_loads(owner_a, owner_b, core, cotangent, block_a, block_b, landed_a, landed_b):
    loads = column_copies(owner_a[0] * C + core, OWN, cotangent, block_a, landed_a)
    return loads + column_copies(owner_b[0] * C + core, OWN, cotangent, block_b, landed_b)


def second_kernel(
    core, behind, ahead, kept, pair, cotangent, out, a, b, mine, landed_a, landed_b, landed
):
    loads = block_loads(ahead, behind, 1 - core[0], cotangent, a, b, landed_a, landed_b)
    loads += column_copies(ahead[0] * C + core[0], OWN, cotangent, mine, landed)
    start_all(loads)
    out[...] = product(kept[...], pair[:, core_columns(core[0])])
    wait_all(loads)


def third_kernel(core, behind, kept, a, b, cotangent, out_a, out_b, mine, landed):
    loads = column_copies(behind[0] * C + core[0], OWN, cotangent, mine, landed)
    start_all(loads)
    out_a[...] = product(kept[...], a[...])
    out_b[...] = product(kept[...], b[...])
    wait_all(loads)


def fourth_kernel(kept, a, b, out_a, out_b):
    out_a[...] = product(kept[...], a[...])
    out_b[...] = product(kept[...], b[...])


def last_kernel(core, owner, kept, cotangent, away, out, pair, landed):
    loads = column_copies(owner[0], C * OWN, cotangent, pair, landed)
    start_all(loads)
    wait_all(loads)
    away[...] = product(kept[...], pair[:, core_columns(1 - core[0])])
    out[...] = product(kept[...], pair[:, core_columns(core[0])])


BLOCK = ((ROWS, OWN), F32)
KEPT = ((DEPTH, ROWS), BF16)
PAIR = ((DEPTH, C * OWN), BF16)
HALF = ((DEPTH, OWN), BF16)


def loading_call(kernel, name, limit, in_specs, outs, semaphores, *operands):
    return pl.pallas_call(
        kernel,
        name=name,
        in_specs=in_specs,
        out_specs=[VMEM] * len(outs),
        out_shape=[jax.ShapeDtypeStruct(shape, kind) for shape, kind in outs],
        scratch_shapes=[pltpu.SemaphoreType.DMA((count,)) for count in semaphores],
        compiler_params=pltpu.CompilerParams(vmem_limit_bytes=limit),
        cost_estimate=NO_COST,
    )(*operands)


def lane_sums(block):
    folded = block[:, :LANES] + block[:, LANES:]
    return jnp.sum(folded.T, axis=0, keepdims=True)


def split_rows(core, first_row, halves, mine, away):
    first = core[0] == 0
    for group in range(SHARE):
        at = first_row + group
        a, b = halves[0][group], halves[1][group]
        mine[at : at + 1, :] = jnp.where(first, a, b)
        away[at : at + 1, :] = jnp.where(first, b, a)


def gradient_rows(gradient, half, group):
    at = (half * SHARE + group) * LANES
    return gradient[at : at + LANES, :]


def square_rows_kernel(core, gradient, param, mine, away):
    halves = []
    for half in range(C):
        blocks = [gradient_rows(gradient, half, group) for group in range(SHARE)]
        halves.append([lane_sums(block * block) for block in blocks])
    split_rows(core, 0, halves, mine, away)
    value = param[...]
    total = jnp.full((SHARE, LANES), jnp.sum(value * value))
    mine[SHARE:, :] = total
    away[SHARE:, :] = total


def column_state(col_a, col_b, col_state):
    return decay_rate * col_state[...] + (1.0 - decay_rate) * (col_a[...] + col_b[...]) / D


def weighted_rows_kernel(core, gradient, col_a, col_b, col_state, mine_in, away_in, mine, away):
    inverse = 1.0 / column_state(col_a, col_b, col_state)
    halves = []
    for half in range(C):
        blocks = [gradient_rows(gradient, half, group) for group in range(SHARE)]
        halves.append([lane_sums(block * block * inverse) for block in blocks])
    split_rows(core, 2 * SHARE, halves, mine, away)
    mine[: 2 * SHARE, :] = mine_in[...]
    away[: 2 * SHARE, :] = away_in[...]
    mine[3 * SHARE :, :] = jnp.zeros((SHARE, LANES), F32)
    away[3 * SHARE :, :] = jnp.zeros((SHARE, LANES), F32)


def message_kernel(mine, came, out):
    packed = mine[...] + came[...]
    high = packed.astype(BF16)
    rest = (packed - high.astype(F32)).astype(BF16)
    pieces = [
        high[:SHARE],
        rest[:SHARE],
        high[2 * SHARE : 3 * SHARE],
        high[SHARE : SHARE + 2],
        rest[SHARE : SHARE + 2],
    ]
    message = jnp.concatenate([piece.astype(F32) for piece in pieces], axis=0).astype(BF16)
    for k in range(Y * Z):
        out[k] = message


def reduce_kernel(core, came, row_state, out):
    total = jnp.sum(came[...].astype(F32), axis=0)
    squares = total[:SHARE] + total[SHARE : 2 * SHARE]
    weighted = total[2 * SHARE : 3 * SHARE]
    state = jnp.where(core[0] == 0, row_state[:SHARE, :], row_state[SHARE:, :])
    row = decay_rate * state + (1.0 - decay_rate) * squares / FF
    param_total = total[3 * SHARE : 3 * SHARE + 1] + total[3 * SHARE + 2 : 3 * SHARE + 3]
    out[:SHARE, :] = row
    out[SHARE : SHARE + 1, :] = jnp.full((1, LANES), jnp.sum(weighted / row))
    out[SHARE + 1 : SHARE + 2, :] = jnp.full((1, LANES), jnp.sum(row))
    out[SHARE + 2 :, :] = jnp.broadcast_to(0.5 * param_total, (2, LANES))


def whole_rows(core, mine, twin):
    first = core[0] == 0
    a, b = mine[:SHARE, :], twin[:SHARE, :]
    return jnp.concatenate([jnp.where(first, a, b), jnp.where(first, b, a)], axis=0)


def normalise_kernel(
    core, gradient, mine, twin, col_a, col_b, col_state, update, new_row, new_col
):
    col = column_state(col_a, col_b, col_state)
    row = whole_rows(core, mine, twin)
    new_col[...] = col
    new_row[...] = row
    col_factor = lax.rsqrt(col)
    row_factor = lax.rsqrt(row)
    for group in range(GROUPS):
        block = gradient[group * LANES : (group + 1) * LANES, :]
        along = jnp.broadcast_to(row_factor[group : group + 1, :], (LANES, LANES)).T
        factor = jnp.concatenate([along, along], axis=1) * col_factor
        update[group * LANES : (group + 1) * LANES, :] = block * factor


def step_kernel(scalars_a, scalars_b, param, update, new_param, stage, sent):
    sums = scalars_a[...] + scalars_b[...]
    entries = D * FF
    row_level = sums[SHARE + 1 : SHARE + 2] / D
    clip = jnp.maximum(1.0, jnp.sqrt(row_level * sums[SHARE : SHARE + 1] / entries))
    scale = jnp.sqrt(sums[SHARE + 2 : SHARE + 3] / entries)
    factor = step_size * scale * jnp.sqrt(row_level) / clip
    factor = jnp.concatenate([factor, factor], axis=1)
    copies = []
    for group in range(GROUPS):
        rows = pl.ds(group * LANES, LANES)
        stage[rows, :] = param[rows, :] - factor * update[rows, :]
        copy = pltpu.make_async_copy(stage.at[rows, :], new_param.at[rows, :], sent.at[group])
        copy.start()
        copies.append(copy)
    wait_all(copies)


def per_device(activations, cotangent, param, row_state, col_state):
    y = lax.axis_index("y")
    c = lax.axis_index("c")
    barrier = lax.optimization_barrier
    way = 2 * c - 1
    hops = [lax.rem(y + Y + hop, Y)[None] for hop in (2, -way, way, 0)]
    *hops, core = barrier((*hops, c[None]))

    def wide(value):
        return value.astype(F32)

    def narrow(value):
        return barrier(value.astype(WIRE))

    def swapped(value, count):
        cuts = [ROWS * k // count // 16 * 16 for k in range(count + 1)]
        parts = [narrow(value[a:b]) for a, b in zip(cuts, cuts[1:])]
        parts = [lax.ppermute(part, "c", swap_core) for part in parts]
        return wide(jnp.concatenate(parts))

    far_away, kept, pair = loading_call(
        first_kernel,
        "first_matmul",
        FIRST_LIMIT,
        [SMEM, SMEM, HBM, HBM],
        [BLOCK, KEPT, PAIR],
        [STEPS, STEPS],
        hops[0],
        core,
        activations,
        cotangent,
    )
    far_came = lax.ppermute(far_away, "c", swap_core)
    far, away_a, away_b, mine_b = loading_call(
        second_kernel,
        "second_matmul",
        SECOND_LIMIT,
        [SMEM, SMEM, SMEM, VMEM, VMEM, HBM],
        [BLOCK, HALF, HALF, HALF],
        [STEPS] * 3,
        core,
        hops[1],
        hops[2],
        kept,
        pair,
        cotangent,
    )
    far = narrow(far + far_came)
    far_sent = lax.ppermute(far, ("y", "c"), to_ahead)

    away_a, _ = barrier((away_a, far))
    behind_away, ahead_away, mine_a = loading_call(
        third_kernel,
        "third_matmul",
        MIDDLE_LIMIT,
        [SMEM, SMEM, VMEM, VMEM, VMEM, HBM],
        [BLOCK, BLOCK, HALF],
        [STEPS],
        core,
        hops[1],
        kept,
        away_a,
        away_b,
        cotangent,
    )
    behind_came = swapped(behind_away, 3)
    ahead_came = swapped(ahead_away, 1)
    behind, ahead = call(fourth_kernel, "fourth_matmul", [BLOCK, BLOCK], kept, mine_a, mine_b)
    behind = narrow(behind + behind_came)
    behind_sent = lax.ppermute(behind, ("y", "c"), to_behind)
    ahead, _ = barrier((ahead, behind))
    ahead = narrow(ahead + ahead_came + wide(far_sent))
    ahead_sent = lax.ppermute(ahead, ("y", "c"), to_ahead)

    kept, _ = barrier((kept, ahead))
    own_away, own = pl.pallas_call(
        last_kernel,
        name="last_matmul",
        in_specs=[SMEM, SMEM, VMEM, HBM],
        out_specs=[VMEM, VMEM],
        out_shape=[jax.ShapeDtypeStruct(*BLOCK)] * 2,
        scratch_shapes=[pltpu.VMEM(*PAIR), pltpu.SemaphoreType.DMA((STEPS,))],
        compiler_params=pltpu.CompilerParams(vmem_limit_bytes=LAST_LIMIT),
        cost_estimate=NO_COST,
    )(core, hops[3], kept, cotangent)
    own_came = swapped(own_away, 2)
    gradient = own + own_came + wide(behind_sent) + wide(ahead_sent)

    col_part = jnp.sum(gradient * gradient, axis=0)
    col_part = col_part.reshape(1, OWN)
    col_came = (
        lax.ppermute(col_part, "x", pair_near)
        + lax.ppermute(col_part, "x", pair_wrap)
        + lax.ppermute(col_part, "x", pair_cross)
    )
    mine, away = call(
        square_rows_kernel, "square_rows", [TILE32, TILE32], core, gradient, param, scalars=1
    )
    columns = (col_part, col_came, col_state.reshape(1, OWN))
    mine, away = call(
        weighted_rows_kernel,
        "weighted_rows",
        [((2 * 8, LANES), F32), ((2 * 8, LANES), F32)],
        core,
        gradient,
        *columns,
        mine,
        away,
        scalars=1,
    )
    came = lax.ppermute(away, "c", swap_core)
    (message,) = call(message_kernel, "message", [((Y * Z, 16, LANES), BF16)], mine, came)
    came = lax.all_to_all(message, ("y", "z"), 0, 0, tiled=True)
    (reduced,) = call(
        reduce_kernel,
        "row_reduce",
        [TILE32],
        core,
        came,
        row_state.reshape(TILE),
        scalars=1,
    )
    twin = lax.ppermute(reduced, "c", swap_core)
    scalars = reduced + twin
    scalars_came = (
        lax.ppermute(scalars, "x", pair_near)
        + lax.ppermute(scalars, "x", pair_wrap)
        + lax.ppermute(scalars, "x", pair_cross)
    )
    update, new_row, new_col = call(
        normalise_kernel,
        "normalise",
        [BLOCK, TILE32, ((1, OWN), F32)],
        core,
        gradient,
        reduced,
        twin,
        *columns,
        scalars=1,
    )
    new_param = pl.pallas_call(
        step_kernel,
        name="step",
        in_specs=[VMEM] * 4,
        out_specs=HBM,
        out_shape=jax.ShapeDtypeStruct((ROWS, OWN), F32),
        scratch_shapes=[pltpu.VMEM((ROWS, OWN), F32), pltpu.SemaphoreType.DMA((GROUPS,))],
        compiler_params=pltpu.CompilerParams(vmem_limit_bytes=LIMIT),
        cost_estimate=NO_COST,
    )(scalars, scalars_came, param, update)
    return (new_param, new_row.reshape(ROWS), new_col.reshape(OWN))


def solution(mesh):
    split = Mesh(mesh.devices.reshape(Y, C, X, Z), ("y", "c", "x", "z"))
    tokens = ("y", "c")
    columns = ("z", "y", "c")
    in_specs = (P(tokens, "x"), P(tokens, "z"), P("x", columns), P("x"), P(columns))
    out_specs = (P("x", columns), P("x"), P(columns))
    return jax.shard_map(
        per_device, mesh=split, in_specs=in_specs, out_specs=out_specs, check_vma=False
    )
```

```python
import jax
import jax.numpy as jnp
from jax import lax
from jax.experimental import pallas as pl
from jax.experimental.pallas import tpu as pltpu
from jax.sharding import Mesh, PartitionSpec as P

D = 4096
FF = 16384
TOKENS = 12288

decay_rate = 0.9
step_size = 0.3

Y, C, X, Z = 4, 2, 4, 8
ROWS = D // X
OWN = FF // (Z * Y * C)
DEPTH = TOKENS // (Y * C)
LANES = 128
GROUPS = ROWS // LANES
SHARE = GROUPS // C
STEPS = 6
WIRE = jnp.float16
F32 = jnp.float32
BF16 = jnp.bfloat16
TILE = (8, LANES)
TILE32 = (TILE, F32)

swap_core = [(0, 1), (1, 0)]
turn = (-1, 1)
to_ahead = [(i * C + k, (i + turn[k]) % Y * C + k) for i in range(Y) for k in range(C)]
to_behind = [(i * C + k, (i - turn[k]) % Y * C + k) for i in range(Y) for k in range(C)]
pair_near = [(i, i ^ 1) for i in range(X)]
pair_wrap = [(i, X - 1 - i) for i in range(X)]
pair_cross = [(i, (i + 2) % X) for i in range(X)]

VMEM = pl.BlockSpec(memory_space=pltpu.VMEM)
SMEM = pl.BlockSpec(memory_space=pltpu.SMEM)
HBM = pl.BlockSpec(memory_space=pltpu.HBM)
LIMIT = 14 * 2**20
FIRST_LIMIT = 48 * 2**20
SECOND_LIMIT = 43 * 2**20
LAST_LIMIT = 43 * 2**20
MIDDLE_LIMIT = 42 * 2**20
NO_COST = pl.CostEstimate(flops=1, bytes_accessed=1, transcendentals=0)


def call(kernel, name, outs, *operands, scalars=0):
    return pl.pallas_call(
        kernel,
        name=name,
        in_specs=[SMEM] * scalars + [VMEM] * (len(operands) - scalars),
        out_specs=[VMEM] * len(outs),
        out_shape=[jax.ShapeDtypeStruct(shape, kind) for shape, kind in outs],
        compiler_params=pltpu.CompilerParams(vmem_limit_bytes=LIMIT),
        cost_estimate=NO_COST,
    )(*operands)


def load_rows(k):
    return pl.ds(k * DEPTH // STEPS, DEPTH // STEPS)


def column_copies(place, width, cotangent, block, landed):
    columns = pl.ds(pl.multiple_of(place * width, width), width)
    return [
        pltpu.make_async_copy(
            cotangent.at[load_rows(k), columns], block.at[load_rows(k), :], landed.at[k]
        )
        for k in range(STEPS)
    ]


def start_all(copies):
    for copy in copies:
        copy.start()


def wait_all(copies):
    for copy in copies:
        copy.wait()


def product(left, right):
    return lax.dot_general(left, right, (((0,), (0,)), ((), ())), preferred_element_type=F32)


def core_columns(core):
    return pl.ds(pl.multiple_of(core * OWN, OWN), OWN)


def first_kernel(owner, core, activations, cotangent, out, kept, pair, arrived, landed):
    blocks = column_copies(owner[0], C * OWN, cotangent, pair, landed)
    wholes = [
        pltpu.make_async_copy(
            activations.at[load_rows(k), :], kept.at[load_rows(k), :], arrived.at[k]
        )
        for k in range(STEPS)
    ]
    for block, whole in zip(blocks, wholes):
        block.start()
        whole.start()
    away = core_columns(1 - core[0])
    group = STEPS // 3
    for k in range(0, STEPS, group):
        wait_all(blocks[k : k + group] + wholes[k : k + group])
        rows = pl.ds(k * DEPTH // STEPS, group * DEPTH // STEPS)
        value = product(kept[rows, :], pair[rows, away])
        if k == 0:
            out[...] = value
        else:
            out[...] += value


def block_loads(owner_a, owner_b, core, cotangent, block_a, block_b, landed_a, landed_b):
    loads = column_copies(owner_a[0] * C + core, OWN, cotangent, block_a, landed_a)
    return loads + column_copies(owner_b[0] * C + core, OWN, cotangent, block_b, landed_b)


def second_kernel(
    core, behind, ahead, kept, pair, cotangent, out, a, b, mine, landed_a, landed_b, landed
):
    loads = block_loads(ahead, behind, 1 - core[0], cotangent, a, b, landed_a, landed_b)
    loads += column_copies(ahead[0] * C + core[0], OWN, cotangent, mine, landed)
    start_all(loads)
    out[...] = product(kept[...], pair[:, core_columns(core[0])])
    wait_all(loads)


def third_kernel(core, behind, kept, a, b, cotangent, out_a, out_b, mine, landed):
    loads = column_copies(behind[0] * C + core[0], OWN, cotangent, mine, landed)
    start_all(loads)
    out_a[...] = product(kept[...], a[...])
    out_b[...] = product(kept[...], b[...])
    wait_all(loads)


def fourth_kernel(kept, a, b, out_a, out_b):
    out_a[...] = product(kept[...], a[...])
    out_b[...] = product(kept[...], b[...])


def last_kernel(core, owner, kept, cotangent, away, out, pair, landed):
    loads = column_copies(owner[0], C * OWN, cotangent, pair, landed)
    start_all(loads)
    wait_all(loads)
    away[...] = product(kept[...], pair[:, core_columns(1 - core[0])])
    out[...] = product(kept[...], pair[:, core_columns(core[0])])


BLOCK = ((ROWS, OWN), F32)
KEPT = ((DEPTH, ROWS), BF16)
PAIR = ((DEPTH, C * OWN), BF16)
HALF = ((DEPTH, OWN), BF16)


def loading_call(kernel, name, limit, in_specs, outs, semaphores, *operands):
    return pl.pallas_call(
        kernel,
        name=name,
        in_specs=in_specs,
        out_specs=[VMEM] * len(outs),
        out_shape=[jax.ShapeDtypeStruct(shape, kind) for shape, kind in outs],
        scratch_shapes=[pltpu.SemaphoreType.DMA((count,)) for count in semaphores],
        compiler_params=pltpu.CompilerParams(vmem_limit_bytes=limit),
        cost_estimate=NO_COST,
    )(*operands)


def lane_sums(block):
    folded = block[:, :LANES] + block[:, LANES:]
    return jnp.sum(folded.T, axis=0, keepdims=True)


def split_rows(core, first_row, halves, mine, away):
    first = core[0] == 0
    for group in range(SHARE):
        at = first_row + group
        a, b = halves[0][group], halves[1][group]
        mine[at : at + 1, :] = jnp.where(first, a, b)
        away[at : at + 1, :] = jnp.where(first, b, a)


def gradient_rows(gradient, half, group):
    at = (half * SHARE + group) * LANES
    return gradient[at : at + LANES, :]


def square_rows_kernel(core, gradient, param, mine, away):
    halves = []
    for half in range(C):
        blocks = [gradient_rows(gradient, half, group) for group in range(SHARE)]
        halves.append([lane_sums(block * block) for block in blocks])
    split_rows(core, 0, halves, mine, away)
    value = param[...]
    total = jnp.full((SHARE, LANES), jnp.sum(value * value))
    mine[SHARE:, :] = total
    away[SHARE:, :] = total


def column_state(col_a, col_b, col_state):
    return decay_rate * col_state[...] + (1.0 - decay_rate) * (col_a[...] + col_b[...]) / D


def weighted_rows_kernel(core, gradient, col_a, col_b, col_state, mine_in, away_in, mine, away):
    inverse = 1.0 / column_state(col_a, col_b, col_state)
    halves = []
    for half in range(C):
        blocks = [gradient_rows(gradient, half, group) for group in range(SHARE)]
        halves.append([lane_sums(block * block * inverse) for block in blocks])
    split_rows(core, 2 * SHARE, halves, mine, away)
    mine[: 2 * SHARE, :] = mine_in[...]
    away[: 2 * SHARE, :] = away_in[...]
    mine[3 * SHARE :, :] = jnp.zeros((SHARE, LANES), F32)
    away[3 * SHARE :, :] = jnp.zeros((SHARE, LANES), F32)


def message_kernel(mine, came, out):
    packed = mine[...] + came[...]
    high = packed.astype(BF16)
    rest = (packed - high.astype(F32)).astype(BF16)
    pieces = [
        high[:SHARE],
        rest[:SHARE],
        high[2 * SHARE : 3 * SHARE],
        high[SHARE : SHARE + 2],
        rest[SHARE : SHARE + 2],
    ]
    message = jnp.concatenate([piece.astype(F32) for piece in pieces], axis=0).astype(BF16)
    for k in range(Y * Z):
        out[k] = message


def reduce_kernel(core, came, row_state, out):
    total = jnp.sum(came[...].astype(F32), axis=0)
    squares = total[:SHARE] + total[SHARE : 2 * SHARE]
    weighted = total[2 * SHARE : 3 * SHARE]
    state = jnp.where(core[0] == 0, row_state[:SHARE, :], row_state[SHARE:, :])
    row = decay_rate * state + (1.0 - decay_rate) * squares / FF
    param_total = total[3 * SHARE : 3 * SHARE + 1] + total[3 * SHARE + 2 : 3 * SHARE + 3]
    out[:SHARE, :] = row
    out[SHARE : SHARE + 1, :] = jnp.full((1, LANES), jnp.sum(weighted / row))
    out[SHARE + 1 : SHARE + 2, :] = jnp.full((1, LANES), jnp.sum(row))
    out[SHARE + 2 :, :] = jnp.broadcast_to(0.5 * param_total, (2, LANES))


def whole_rows(core, mine, twin):
    first = core[0] == 0
    a, b = mine[:SHARE, :], twin[:SHARE, :]
    return jnp.concatenate([jnp.where(first, a, b), jnp.where(first, b, a)], axis=0)


def normalise_kernel(
    core, gradient, mine, twin, col_a, col_b, col_state, update, new_row, new_col
):
    col = column_state(col_a, col_b, col_state)
    row = whole_rows(core, mine, twin)
    new_col[...] = col
    new_row[...] = row
    col_factor = lax.rsqrt(col)
    row_factor = lax.rsqrt(row)
    for group in range(GROUPS):
        block = gradient[group * LANES : (group + 1) * LANES, :]
        along = jnp.broadcast_to(row_factor[group : group + 1, :], (LANES, LANES)).T
        factor = jnp.concatenate([along, along], axis=1) * col_factor
        update[group * LANES : (group + 1) * LANES, :] = block * factor


def step_kernel(scalars_a, scalars_b, param, update, new_param, stage, sent):
    sums = scalars_a[...] + scalars_b[...]
    entries = D * FF
    row_level = sums[SHARE + 1 : SHARE + 2] / D
    clip = jnp.maximum(1.0, jnp.sqrt(row_level * sums[SHARE : SHARE + 1] / entries))
    scale = jnp.sqrt(sums[SHARE + 2 : SHARE + 3] / entries)
    factor = step_size * scale * jnp.sqrt(row_level) / clip
    factor = jnp.concatenate([factor, factor], axis=1)
    copies = []
    for group in range(GROUPS // 2):
        rows = pl.ds(group * 2 * LANES, 2 * LANES)
        stage[rows, :] = param[rows, :] - factor * update[rows, :]
        copy = pltpu.make_async_copy(stage.at[rows, :], new_param.at[rows, :], sent.at[group])
        copy.start()
        copies.append(copy)
    wait_all(copies)


def per_device(activations, cotangent, param, row_state, col_state):
    y = lax.axis_index("y")
    c = lax.axis_index("c")
    barrier = lax.optimization_barrier
    way = 2 * c - 1
    hops = [lax.rem(y + Y + hop, Y)[None] for hop in (2, -way, way, 0)]
    *hops, core = barrier((*hops, c[None]))

    def wide(value):
        return value.astype(F32)

    def narrow(value):
        return barrier(value.astype(WIRE))

    def swapped(value, count):
        cuts = [ROWS * k // count // 16 * 16 for k in range(count + 1)]
        parts = [narrow(value[a:b]) for a, b in zip(cuts, cuts[1:])]
        parts = [lax.ppermute(part, "c", swap_core) for part in parts]
        return wide(jnp.concatenate(parts))

    far_away, kept, pair = loading_call(
        first_kernel,
        "first_matmul",
        FIRST_LIMIT,
        [SMEM, SMEM, HBM, HBM],
        [BLOCK, KEPT, PAIR],
        [STEPS, STEPS],
        hops[0],
        core,
        activations,
        cotangent,
    )
    far_came = lax.ppermute(far_away, "c", swap_core)
    far, away_a, away_b, mine_b = loading_call(
        second_kernel,
        "second_matmul",
        SECOND_LIMIT,
        [SMEM, SMEM, SMEM, VMEM, VMEM, HBM],
        [BLOCK, HALF, HALF, HALF],
        [STEPS] * 3,
        core,
        hops[1],
        hops[2],
        kept,
        pair,
        cotangent,
    )
    far = narrow(far + far_came)
    far_sent = lax.ppermute(far, ("y", "c"), to_ahead)

    away_a, _ = barrier((away_a, far))
    behind_away, ahead_away, mine_a = loading_call(
        third_kernel,
        "third_matmul",
        MIDDLE_LIMIT,
        [SMEM, SMEM, VMEM, VMEM, VMEM, HBM],
        [BLOCK, BLOCK, HALF],
        [STEPS],
        core,
        hops[1],
        kept,
        away_a,
        away_b,
        cotangent,
    )
    behind_came = swapped(behind_away, 3)
    ahead_came = swapped(ahead_away, 1)
    behind, ahead = call(fourth_kernel, "fourth_matmul", [BLOCK, BLOCK], kept, mine_a, mine_b)
    behind = narrow(behind + behind_came)
    behind_sent = lax.ppermute(behind, ("y", "c"), to_behind)
    ahead, _ = barrier((ahead, behind))
    ahead = narrow(ahead + ahead_came + wide(far_sent))
    ahead_sent = lax.ppermute(ahead, ("y", "c"), to_ahead)

    kept, _ = barrier((kept, ahead))
    own_away, own = pl.pallas_call(
        last_kernel,
        name="last_matmul",
        in_specs=[SMEM, SMEM, VMEM, HBM],
        out_specs=[VMEM, VMEM],
        out_shape=[jax.ShapeDtypeStruct(*BLOCK)] * 2,
        scratch_shapes=[pltpu.VMEM(*PAIR), pltpu.SemaphoreType.DMA((STEPS,))],
        compiler_params=pltpu.CompilerParams(vmem_limit_bytes=LAST_LIMIT),
        cost_estimate=NO_COST,
    )(core, hops[3], kept, cotangent)
    own_came = swapped(own_away, 2)
    gradient = own + own_came + wide(behind_sent) + wide(ahead_sent)

    col_part = jnp.sum(gradient * gradient, axis=0)
    col_part = col_part.reshape(1, OWN)
    col_came = (
        lax.ppermute(col_part, "x", pair_near)
        + lax.ppermute(col_part, "x", pair_wrap)
        + lax.ppermute(col_part, "x", pair_cross)
    )
    mine, away = call(
        square_rows_kernel, "square_rows", [TILE32, TILE32], core, gradient, param, scalars=1
    )
    columns = (col_part, col_came, col_state.reshape(1, OWN))
    mine, away = call(
        weighted_rows_kernel,
        "weighted_rows",
        [((2 * 8, LANES), F32), ((2 * 8, LANES), F32)],
        core,
        gradient,
        *columns,
        mine,
        away,
        scalars=1,
    )
    came = lax.ppermute(away, "c", swap_core)
    (message,) = call(message_kernel, "message", [((Y * Z, 16, LANES), BF16)], mine, came)
    came = lax.all_to_all(message, ("y", "z"), 0, 0, tiled=True)
    (reduced,) = call(
        reduce_kernel,
        "row_reduce",
        [TILE32],
        core,
        came,
        row_state.reshape(TILE),
        scalars=1,
    )
    twin = lax.ppermute(reduced, "c", swap_core)
    scalars = reduced + twin
    scalars_came = (
        lax.ppermute(scalars, "x", pair_near)
        + lax.ppermute(scalars, "x", pair_wrap)
        + lax.ppermute(scalars, "x", pair_cross)
    )
    update, new_row, new_col = call(
        normalise_kernel,
        "normalise",
        [BLOCK, TILE32, ((1, OWN), F32)],
        core,
        gradient,
        reduced,
        twin,
        *columns,
        scalars=1,
    )
    new_param = pl.pallas_call(
        step_kernel,
        name="step",
        in_specs=[VMEM] * 4,
        out_specs=HBM,
        out_shape=jax.ShapeDtypeStruct((ROWS, OWN), F32),
        scratch_shapes=[pltpu.VMEM((ROWS, OWN), F32), pltpu.SemaphoreType.DMA((GROUPS,))],
        compiler_params=pltpu.CompilerParams(vmem_limit_bytes=LIMIT),
        cost_estimate=NO_COST,
    )(scalars, scalars_came, param, update)
    return (new_param, new_row.reshape(ROWS), new_col.reshape(OWN))


def solution(mesh):
    split = Mesh(mesh.devices.reshape(Y, C, X, Z), ("y", "c", "x", "z"))
    tokens = ("y", "c")
    columns = ("z", "y", "c")
    in_specs = (P(tokens, "x"), P(tokens, "z"), P("x", columns), P("x"), P(columns))
    out_specs = (P("x", columns), P("x"), P(columns))
    return jax.shard_map(
        per_device, mesh=split, in_specs=in_specs, out_specs=out_specs, check_vma=False
    )
```
